256 devices in a mesh: shot: 16 (over z, y_lo), xy: 16 (over y_hi, x, core).
Axes of the slice: x: 4, y: 4 (y_hi: 2, y_lo: 2; y = y_hi * 2 + y_lo), z: 8, core: 2. Of those that a mesh axis runs over, the one named last changes fastest.
Arguments:
- fwd_prev: float32 [16, 128, 512, 128], P('shot', 'xy'), may hold values from -6 to 6
- fwd_cur: float32 [16, 128, 512, 128], P('shot', 'xy'), may hold values from -6 to 6
- bwd_next: float32 [16, 128, 512, 128], P('shot', 'xy'), may hold values from -6 to 6
- bwd_cur: float32 [16, 128, 512, 128], P('shot', 'xy'), may hold values from -6 to 6
- receiver_data: float32 [16, 7, 128, 512], P('shot', None, 'xy'), may hold values from -12 to 12
- velocity_term: float32 [128, 512, 128], P('xy'), may hold values from 0.05 to 0.25
- anisotropy: float32 [128, 512, 128], P('xy'), may hold values from 0 to 0.3
- wavelet: float32 [16, 7], replicated, may hold values from -16 to 16
- shot_x: int32 [16], replicated, may hold values from 0 to 127
- shot_y: int32 [16], replicated, may hold values from 0 to 511
- aperture: int32 [16, 8], replicated, may hold values from 0 to 15, all different within a row
- snap_steps: int32 [4], replicated, may hold values from 1 to 8, as said below
Outputs:
- image: float32 [128, 512, 128], P('xy', 'shot')
The draws below stay inside these ranges and needn't reach their ends.
Inputs may be any that keep to these rules, and one draw needn't show every extreme that they name: `snap_steps`: 4 distinct increasing times; the last is 8. `aperture`: each row names 8 distinct tiles.
All inputs are finite; a program needn't handle non-finite values.
Results may differ from the reference program's by a relative error of at most 0.0021.
Values may be sent and summed in bfloat16 or wider, within the bound.
A program may use at most 128 MiB of HBM per device.

```python
import math
import jax
import jax.numpy as jnp
from jax import lax

CX = 8
NY = 512
NZ = 128
STEPS = 8
NSNAP = 4
SHOTS = 16
NX = 128
APER = 8
N_XY = 16


def draw_snap_steps(key, part):
    chosen = jax.random.permutation(key, STEPS - 1)[:NSNAP - 1] + 1
    joined = jnp.concatenate([chosen.astype(jnp.int32), jnp.full((1,), STEPS, jnp.int32)])
    return jnp.sort(joined).astype(jnp.int32)


def place_ends(result, stream_key, least, top_value):
    shape = result.shape
    place = [jax.random.randint(jax.random.fold_in(stream_key, axis), (), 0, shape[axis]) for axis in range(len(shape))]
    result = result.at[tuple(place)].set(least)
    longest = shape.index(max(shape))
    place[longest] = (place[longest] + 1) % shape[longest]
    return result.at[tuple(place)].set(top_value)


def shard_levels(key, extent, pieces, low, top_value):
    def one(axis_at, blocks):
        draws = jax.random.uniform(jax.random.fold_in(jax.random.fold_in(key, 6), axis_at), (blocks,), jnp.float32, low / len(pieces), top_value / len(pieces))
        return jnp.repeat(jnp.exp(draws), extent[axis_at] // blocks).reshape((-1,) + (1,) * (len(extent) - axis_at - 1))

    gain = one(*pieces[0])
    for cut in pieces[1:]:
        gain = gain * one(*cut)
    return gain


def different_ones(key, rows, count, top, lift):
    ranking = jax.random.permutation(jax.random.fold_in(key, 1), count)
    boost = ranking
    for power in range(3):
        boost = boost * boost // count
    boost = boost * lift // count
    tickets = jax.random.randint(jax.random.fold_in(key, 2), (rows, count), 0, 4096) + boost
    holders = jax.random.permutation(jax.random.fold_in(key, 3), rows)[jnp.arange(count) % rows]
    tickets = jnp.where(jnp.arange(rows)[:, None] == holders[None, :], 1 << 14, tickets)
    score = tickets * count + jnp.arange(count)
    return lax.top_k(score.astype(jnp.int32), top)[1].astype(jnp.int32)


def gaussian(rng, shape, scale, reach, split=(), kind=jnp.bfloat16):
    drawn = jax.random.normal(rng, shape, jnp.float32) * scale
    if len(split) > 0:
        drawn = shard_levels(rng, shape, split, -0.22, 0.18) * drawn
    return jnp.clip(drawn, min=-reach, max=reach).astype(kind)


def setup_inputs(seed: int = 0) -> dict:
    keys = jax.random.split(jax.random.key(seed), 13)
    fwd_prev = gaussian(keys[0], (SHOTS, NX, NY, NZ), 1.0, 6.0, ((0, 16), (1, 16)), jnp.float32)
    fwd_cur = gaussian(keys[1], (SHOTS, NX, NY, NZ), 1.0, 6.0, ((0, 16), (1, 16)), jnp.float32)
    bwd_next = gaussian(keys[2], (SHOTS, NX, NY, NZ), 1.0, 6.0, ((0, 16), (1, 16)), jnp.float32)
    bwd_cur = gaussian(keys[3], (SHOTS, NX, NY, NZ), 1.0, 6.0, ((0, 16), (1, 16)), jnp.float32)
    receiver_data = gaussian(keys[4], (SHOTS, STEPS - 1, NX, NY), 2.0, 12.0, ((0, 16), (2, 16)), jnp.float32)
    velocity_term = jnp.clip(jnp.exp(math.log(0.25) - 1.609438 * jax.random.uniform(keys[5], (NX, NY, NZ), jnp.float32) ** shard_levels(keys[5], (NX, NY, NZ), ((0, 16),), -0.2, 0.2)), 0.05, 0.25)
    anisotropy = jnp.clip(0.3 * jax.random.uniform(keys[6], (NX, NY, NZ), jnp.float32) ** shard_levels(keys[6], (NX, NY, NZ), ((0, 16),), -0.2, 0.2), 0.0, 0.3)
    wavelet = gaussian(keys[7], (SHOTS, STEPS - 1), 4.0, 16.0, (), jnp.float32)
    shot_x = place_ends(jax.random.randint(keys[8], (SHOTS,), 0, NX), jax.random.fold_in(keys[8], 1), 0, NX - 1).astype(jnp.int32)
    shot_y = place_ends(jax.random.randint(keys[9], (SHOTS,), 0, NY), jax.random.fold_in(keys[9], 1), 0, NY - 1).astype(jnp.int32)
    aperture = different_ones(keys[10], SHOTS, N_XY, APER, 8192)
    snap_steps = draw_snap_steps(jax.random.fold_in(keys[12], 71), 0)
    return {"fwd_prev": fwd_prev, "fwd_cur": fwd_cur, "bwd_next": bwd_next, "bwd_cur": bwd_cur, "receiver_data": receiver_data, "velocity_term": velocity_term, "anisotropy": anisotropy, "wavelet": wavelet, "shot_x": shot_x, "shot_y": shot_y, "aperture": aperture, "snap_steps": snap_steps}


def laplace(field, horizontal):
    padded = jnp.pad(field, 1)
    lateral = padded[2:, 1:-1, 1:-1] + padded[:-2, 1:-1, 1:-1] + padded[1:-1, 2:, 1:-1] + padded[1:-1, :-2, 1:-1] - 4.0 * field
    vertical = padded[1:-1, 1:-1, 2:] + padded[1:-1, 1:-1, :-2] - 2.0 * field
    return horizontal * lateral + vertical


def reference(fwd_prev, fwd_cur, bwd_next, bwd_cur, receiver_data, velocity_term, anisotropy, wavelet, shot_x, shot_y, aperture, snap_steps):
    horizontal = 1.0 + 2.0 * anisotropy
    surface = velocity_term[:, :, 0]
    slots = jnp.arange(NSNAP, dtype=jnp.int32)
    tile_of = (jnp.arange(NX, dtype=jnp.int32) // CX).astype(jnp.int32)
    half = SHOTS // 2

    def one_shot(image, shot):
        plane = ((jnp.arange(NX, dtype=jnp.int32) == shot_x[shot])[:, None] & (jnp.arange(NY, dtype=jnp.int32) == shot_y[shot])[None, :]).astype(jnp.float32)
        before = lax.dynamic_index_in_dim(fwd_prev, shot, 0, keepdims=False)
        current = lax.dynamic_index_in_dim(fwd_cur, shot, 0, keepdims=False)
        snaps = jnp.zeros((NSNAP, NX, NY, NZ), jnp.bfloat16)

        def record(snaps, field, time):
            is_hit = snap_steps == time
            found = jnp.any(is_hit)
            slot = jnp.sum(jnp.where(is_hit, slots, 0)).astype(jnp.int32)
            older = lax.dynamic_slice_in_dim(snaps, slot, 1, 0)
            newer = jnp.where(found, field.astype(jnp.bfloat16)[None], older)
            return lax.dynamic_update_slice_in_dim(snaps, newer, slot, 0)

        def forward_step(index, carry):
            before, current, snaps = carry
            snaps = record(snaps, current, index + 1)
            amplitude = wavelet[shot, index]
            after = 2.0 * current - before + velocity_term * laplace(current, horizontal)
            after = after.at[:, :, 0].add(surface * plane * amplitude)
            return current, after, snaps

        before, current, snaps = lax.fori_loop(0, STEPS - 1, forward_step, (before, current, snaps))
        snaps = record(snaps, current, STEPS)

        row = ((shot + half) % SHOTS).astype(jnp.int32)
        later = lax.dynamic_index_in_dim(bwd_next, row, 0, keepdims=False)
        wave = lax.dynamic_index_in_dim(bwd_cur, row, 0, keepdims=False)
        records = lax.dynamic_index_in_dim(receiver_data, row, 0, keepdims=False)

        def correlate(partial_value, field, time):
            is_hit = snap_steps == time
            found = jnp.any(is_hit)
            slot = jnp.sum(jnp.where(is_hit, slots, 0)).astype(jnp.int32)
            taken = lax.dynamic_index_in_dim(snaps, slot, 0, keepdims=False).astype(jnp.float32)
            return partial_value + jnp.where(found, taken * field, 0.0)

        def backward_step(index, carry):
            later, wave, partial_value = carry
            time = STEPS - index
            partial_value = correlate(partial_value, wave, time)
            trace = lax.dynamic_index_in_dim(records, time - 2, 0, keepdims=False)
            earlier = 2.0 * wave - later + velocity_term * laplace(wave, horizontal)
            earlier = earlier.at[:, :, 0].add(surface * trace)
            return wave, earlier, partial_value

        partial_value = jnp.zeros((NX, NY, NZ), jnp.float32)
        later, wave, partial_value = lax.fori_loop(0, STEPS - 1, backward_step, (later, wave, partial_value))
        partial_value = correlate(partial_value, wave, 1)
        inside = jnp.any(tile_of[:, None] == aperture[shot][None, :], axis=1).astype(jnp.float32)
        return image + partial_value * inside[:, None, None], None

    image, unused = lax.scan(one_shot, jnp.zeros((NX, NY, NZ), jnp.float32), jnp.arange(SHOTS, dtype=jnp.int32))
    return image
```

```python
import functools

import jax
import jax.numpy as jnp
from jax import lax
from jax.experimental import pallas as pl
from jax.experimental.pallas import tpu as pltpu
from jax.sharding import PartitionSpec as P

MESH = pl.DeviceIdType.MESH
TOP = 32767.0
BLOCKS = 33
CHUNK = 3
CHUNKS = BLOCKS // CHUNK
ROWS = 8 * BLOCKS
STEPS = 7
WIDE = 22
FIELD_TOP = 6.0
RECORD_TOP = 12.0
SPEED_TOP = 0.25
SHAPE_TOP = 0.3


def root_code(x, top):
    size = jnp.sqrt(jnp.sqrt(jnp.abs(x) * (1.0 / top))) * TOP
    size = jnp.minimum(jnp.round(size), TOP)
    return jnp.where(x < 0.0, -size, size).astype(jnp.int32).astype(jnp.int16)


def root_value(code, top):
    part = code.astype(jnp.int32).astype(jnp.float32) * (1.0 / TOP)
    return (part * part) * (part * jnp.abs(part)) * top


def line_code(x, top):
    return jnp.round(x * (TOP / top)).astype(jnp.int32).astype(jnp.int16)


def line_value(code, top):
    return code.astype(jnp.int32).astype(jnp.float32) * (top / TOP)


def kernel(
    fields0, fields1, fields2, fields3, speed_hbm, shape_hbm, records, wavelet, shot_x, shot_y, aperture, snap_steps,
    out,
    state, slope, speed, snap_u, snap_w, total, stage, z_out, z_in, near, near_in, far_in,
    inject, marks, turned, rec_z, rec_near, rec_z_in, rec_near_in, rec_far_in, sums,
    in_sem, z_send, z_recv, near_send, near_recv, far_send, far_recv,
    rz_send, rz_recv, rn_send, rn_recv, rf_send, rf_recv, sum_send, sum_recv,
):
    fields = (fields0, fields1, fields2, fields3)
    s, q = lax.axis_index("shot"), lax.axis_index("xy")
    half = s // 8
    across = lax.rem(s + 8, 16)
    left, right = lax.rem(q + 15, 16), lax.rem(q + 1, 16)
    sides = ((s, left), (s, right))
    base = pl.multiple_of(248 * half, 8)
    their_base = pl.multiple_of(248 * (1 - half), 8)

    loads = []
    for f in range(4):
        loads.append(pltpu.make_async_copy(fields[f].at[0, :, pl.ds(their_base, ROWS), :], stage.at[f], in_sem.at[f]))
    for f in range(4):
        loads.append(pltpu.make_async_copy(fields[f].at[0, :, pl.ds(base, ROWS), :], state.at[f, pl.ds(7, 8), pl.ds(8, ROWS), :], in_sem.at[4 + f]))
    loads.append(pltpu.make_async_copy(shape_hbm.at[:, pl.ds(base, ROWS), :], slope.at[pl.ds(7, 8)], in_sem.at[8]))
    loads.append(pltpu.make_async_copy(speed_hbm.at[:, pl.ds(base, ROWS), :], speed.at[pl.ds(7, 8)], in_sem.at[9]))
    for load in loads:
        load.start()

    barrier = pltpu.get_barrier_semaphore()
    peers = [(across, q), *sides]
    for k in range(1, 8):
        peers.append((8 * half + lax.rem(s + k, 8), q))
    for peer in peers:
        pl.semaphore_signal(barrier, inc=1, device_id=peer, device_id_type=MESH)

    def remote(src, dst, send, recv, target):
        return pltpu.make_async_remote_copy(
            src_ref=src, dst_ref=dst, send_sem=send, recv_sem=recv, device_id=target, device_id_type=MESH
        )

    def z_copy(j):
        return remote(z_out.at[j], z_in.at[j], z_send.at[j], z_recv.at[j], (across, q))

    def near_copy(j, side):
        return remote(near.at[j], near_in.at[1 - side, j], near_send.at[side, j], near_recv.at[1 - side, j], sides[side])

    def far_copy(j, side):
        return remote(z_in.at[j], far_in.at[1 - side, j], far_send.at[side, j], far_recv.at[1 - side, j], sides[side])

    def arrived(copy_of, j, side):
        return copy_of(j, 1 - side)

    def rec_near_copy(side):
        return remote(rec_near, rec_near_in.at[1 - side], rn_send.at[side], rn_recv.at[1 - side], sides[side])

    def rec_far_copy(side):
        return remote(rec_z_in, rec_far_in.at[1 - side], rf_send.at[side], rf_recv.at[1 - side], sides[side])

    rec_z_copy = remote(rec_z, rec_z_in, rz_send, rz_recv, (across, q))

    for load in loads[:4]:
        load.wait()
    pl.semaphore_wait(barrier, len(peers))

    @pl.loop(0, CHUNKS)
    def _(j):
        for f in range(4):
            for i in range(CHUNK):
                row = pl.multiple_of(8 * (CHUNK * j + i), 8)
                block = stage[f, :, pl.ds(row, 8), :].reshape(64, 128)
                z_out[j, CHUNK * f + i] = root_code(block, FIELD_TOP)
        z_copy(j).start()

    for load in loads[4:]:
        load.wait()

    @pl.loop(0, CHUNKS)
    def _(j):
        for i in range(CHUNK):
            row = pl.multiple_of(8 * (CHUNK * j + i), 8)
            for f in range(4):
                block = state[f, 7:15, pl.ds(row + 8, 8), :].reshape(64, 128)
                near[j, CHUNK * f + i] = root_code(block, FIELD_TOP)
            near[j, CHUNK * 4 + i] = line_code(slope[7:15, pl.ds(row, 8), :].reshape(64, 128), SHAPE_TOP)
            near[j, CHUNK * 5 + i] = line_code(speed[7:15, pl.ds(row, 8), :].reshape(64, 128), SPEED_TOP)
        for side in range(2):
            near_copy(j, side).start()

    marks[...] = jnp.zeros_like(marks)
    for t in range(STEPS):
        for x in range(8):
            marks[x, t : t + 1, :] = records[0, t, x : x + 1, :]
    turned[pl.ds(512, 16)] = jnp.zeros((16, 128), jnp.float32)
    turned[pl.ds(0, 512)] = jnp.transpose(marks[...].reshape(128, 512), (1, 0))

    @pl.loop(0, 17)
    def _(k):
        row = 16 * k
        rec_z[k] = root_code(turned[pl.ds(pl.multiple_of(their_base + row, 8), 16), :], RECORD_TOP)
        rec_near[k] = root_code(turned[pl.ds(pl.multiple_of(base + row, 8), 16), :], RECORD_TOP)

    rec_z_copy.start()
    for side in range(2):
        rec_near_copy(side).start()

    lane = lax.broadcasted_iota(jnp.int32, (8, 128), 1)
    sub = lax.broadcasted_iota(jnp.int32, (8, 128), 0)
    wide_lane = lax.broadcasted_iota(jnp.int32, (16, 128), 1)
    has = (jnp.where(q > 0, 1.0, 0.0), jnp.where(q < 15, 1.0, 0.0))

    def fill_source(shot):
        tag = jnp.zeros((8, 128), jnp.float32)
        for t in range(STEPS):
            tag = jnp.where((lane & 7) == t, wavelet[shot, t], tag)
        at_x = shot_x[shot] - 8 * q + 7
        at_y = shot_y[shot] - base

        @pl.loop(0, BLOCKS)
        def _(k):
            row = pl.multiple_of(8 * k, 8)
            for g in range(2):
                hit = ((sub + row) == at_y) & (((lane >> 3) + 16 * g) == at_x)
                inject[0, g, pl.ds(row, 8), :] = jnp.where(hit, tag, 0.0)

    def fill_records(middle, beside):
        @pl.loop(0, 17)
        def _(k):
            row = pl.multiple_of(16 * k, 8)
            low = pltpu.roll(root_value(beside[0, k], RECORD_TOP), 120, 1) * has[0]
            mid = pltpu.roll(root_value(middle[k], RECORD_TOP), 56, 1)
            high = pltpu.roll(root_value(beside[1, k], RECORD_TOP), 120, 1) * has[1]
            inject[1, 0, pl.ds(row, 16), :] = jnp.where(wide_lane < 56, low, jnp.where(wide_lane < 120, mid, high))
            inject[1, 1, pl.ds(row, 16), :] = high

    for f in range(4):
        state[f, :, 0:8, :] = jnp.zeros((WIDE, 8, 128), jnp.float32)
        state[f, :, ROWS + 8 : ROWS + 16, :] = jnp.zeros((WIDE, 8, 128), jnp.float32)

    def imaged(shot):
        inside = jnp.float32(0.0)
        for i in range(8):
            inside = inside + jnp.where(aperture[shot, i] == q, 1.0, 0.0)
        scale = []
        for t in range(1, 9):
            hit = jnp.float32(0.0)
            for i in range(4):
                hit = hit + jnp.where(snap_steps[i] == t, 1.0, 0.0)
            scale.append(hit * inside)
        return scale

    own_scale, other_scale = imaged(s), imaged(across)

    def rounded(x):
        return x.astype(jnp.bfloat16).astype(jnp.float32)

    def one_step(phase, w, n, k):
        old, now = 2 * w + (n - 1) % 2, 2 * w + n % 2
        entry = n - 1 if w == 0 else STEPS - n
        row = pl.multiple_of(8 * k, 8)
        here = pl.ds(pl.multiple_of(row + 8, 8), 8)
        groups = [(7, 15)] if n == STEPS else [(n, 7), (7, 15), (15, WIDE - n)]
        for x0, x1 in groups:
            count = x1 - x0
            big = state[now, x0 - 1 : x1 + 1, here, :]
            mid = big[1:-1]
            lateral = big[:-2] + big[2:]
            lateral = lateral + state[now, x0:x1, pl.ds(row + 7, 8), :]
            lateral = lateral + state[now, x0:x1, pl.ds(row + 9, 8), :]
            lateral = lateral - 4.0 * mid
            sources = [inject[w, g, pl.ds(row, 8), :] for g in range(2)]
            added = jnp.stack([
                pltpu.roll(sources[x // 16], (128 - 8 * (x % 16) - entry) % 128, 1) for x in range(x0, x1)
            ])
            at = lax.broadcasted_iota(jnp.int32, (count, 8, 128), 2)
            up = jnp.where(at == 0, added, pltpu.roll(mid, 1, 2))
            down = jnp.where(at == 127, 0.0, pltpu.roll(mid, 127, 2))
            twice = 2.0 * mid
            vertical = up + down - twice
            new = twice - state[old, x0:x1, here, :]
            new = new + slope[x0:x1, pl.ds(row, 8), :] * lateral + speed[x0:x1, pl.ds(row, 8), :] * vertical
            state[old, x0:x1, here, :] = new
            if x0 == 7:
                flat = new.reshape(64, 128)
                if phase == 0 and w == 0:
                    snap_u[n, k] = flat.astype(jnp.bfloat16)
                elif phase == 0:
                    snap_w[STEPS - n, k] = flat
                elif w == 0:
                    total[k] += other_scale[n] * rounded(flat) * snap_w[n, k]
                else:
                    level = STEPS - n
                    total[k] += own_scale[level] * flat * snap_u[level, k].astype(jnp.float32)

    def spread(f, rows, low, high, mid=None):
        state[f, 0:7, rows, :] = (root_value(low, FIELD_TOP) * has[0]).reshape(8, 8, 128)[1:8]
        state[f, 15:22, rows, :] = (root_value(high, FIELD_TOP) * has[1]).reshape(8, 8, 128)[0:7]
        if mid is not None:
            mid = root_value(mid, FIELD_TOP)
            state[f, 7:15, rows, :] = mid.reshape(8, 8, 128)
        return mid

    def open_near(j):
        @pl.loop(0, CHUNK)
        def _(i):
            k = CHUNK * j + i
            row = pl.multiple_of(8 * k, 8)
            rows = pl.ds(pl.multiple_of(row + 8, 8), 8)
            for f in range(4):
                spread(f, rows, near_in[0, j, CHUNK * f + i], near_in[1, j, CHUNK * f + i])
            snap_u[0, k] = state[1, 7:15, rows, :].reshape(64, 128).astype(jnp.bfloat16)
            snap_w[STEPS, k] = state[3, 7:15, rows, :].reshape(64, 128)
            for side, cut, into in ((0, slice(1, 8), slice(0, 7)), (1, slice(0, 7), slice(15, 22))):
                tilt = line_value(near_in[side, j, CHUNK * 4 + i], SHAPE_TOP)
                fast = line_value(near_in[side, j, CHUNK * 5 + i], SPEED_TOP) * has[side]
                speed[into, pl.ds(row, 8), :] = fast.reshape(8, 8, 128)[cut]
                slope[into, pl.ds(row, 8), :] = (fast * (1.0 + 2.0 * tilt)).reshape(8, 8, 128)[cut]
            fast = speed[7:15, pl.ds(row, 8), :]
            slope[7:15, pl.ds(row, 8), :] = fast * (1.0 + 2.0 * slope[7:15, pl.ds(row, 8), :])

    def open_far(j):
        @pl.loop(0, CHUNK)
        def _(i):
            k = CHUNK * j + i
            rows = pl.ds(pl.multiple_of(8 * k + 8, 8), 8)
            mids = []
            for f in range(4):
                at = CHUNK * f + i
                mids.append(spread(f, rows, far_in[0, j, at], far_in[1, j, at], z_in[j, at]))
            total[k] = (
                other_scale[0] * rounded(mids[1]) * snap_w[0, k]
                + own_scale[STEPS] * mids[3] * snap_u[STEPS, k].astype(jnp.float32)
            )

    def advance(phase, j):
        for n in range(1, STEPS + 1):
            first = jnp.maximum(CHUNK * j - n, 0)
            last = jnp.where(j == CHUNKS - 1, BLOCKS, jnp.maximum(CHUNK * j + CHUNK - n, 0))
            for w in range(2):
                @pl.loop(first, last)
                def _(k):
                    one_step(phase, w, n, k)

    fill_source(s)
    for side in range(2):
        rec_near_copy(1 - side).wait_recv()
    fill_records(rec_near, rec_near_in)

    @pl.loop(0, CHUNKS)
    def _(j):
        for side in range(2):
            near_copy(j, 1 - side).wait_recv()
        open_near(j)
        advance(0, j)

    rec_z_copy.wait_recv()
    for side in range(2):
        rec_far_copy(side).start()
    fill_source(across)
    for side in range(2):
        rec_far_copy(1 - side).wait_recv()
    fill_records(rec_z_in, rec_far_in)

    @pl.loop(0, CHUNKS + 1)
    def _(j):
        @pl.when(j < CHUNKS)
        def _():
            z_copy(j).wait_recv()
            for side in range(2):
                far_copy(j, side).start()

        @pl.when(j > 0)
        def _():
            for side in range(2):
                far_copy(j - 1, 1 - side).wait_recv()
            open_far(j - 1)
            advance(1, j - 1)

    def sum_copy(k):
        part = lax.rem(s + k, 8)
        src = total.at[pl.ds(half + 4 * part, 4)]
        return remote(src, sums.at[k - 1], sum_send.at[k - 1], sum_recv.at[k - 1], (8 * half + part, q))

    for k in range(1, 8):
        sum_copy(k).start()
    mine = half + 4 * lax.rem(s, 8)
    for k in range(1, 8):
        sum_copy(k).wait_recv()
    for i in range(4):
        value = total[mine + i]
        for k in range(7):
            value = value + sums[k, i]
        out[:, 8 * i : 8 * i + 8, :] = value.reshape(8, 8, 128)

    @pl.loop(0, CHUNKS)
    def _(j):
        z_copy(j).wait_send()
        for side in range(2):
            near_copy(j, side).wait_send()
            far_copy(j, side).wait_send()

    rec_z_copy.wait_send()
    for side in range(2):
        rec_near_copy(side).wait_send()
        rec_far_copy(side).wait_send()
    for k in range(1, 8):
        sum_copy(k).wait_send()


def on_device(*args):
    f32, i16 = jnp.float32, jnp.int16
    dma = pltpu.SemaphoreType.DMA
    fields = (args[0], args[1], args[2], args[3])
    records, speed, shape = args[4], args[5], args[6]
    anywhere, smem = pl.BlockSpec(memory_space=pl.ANY), pl.BlockSpec(memory_space=pltpu.SMEM)
    vmem = pl.BlockSpec(memory_space=pltpu.VMEM)
    return pl.pallas_call(
        kernel,
        out_shape=jax.ShapeDtypeStruct((8, 32, 128), f32),
        in_specs=[anywhere] * 6 + [vmem] + [smem] * 5,
        out_specs=vmem,
        scratch_shapes=[
            pltpu.VMEM((4, WIDE, ROWS + 16, 128), f32),
            pltpu.VMEM((WIDE, ROWS, 128), f32),
            pltpu.VMEM((WIDE, ROWS, 128), f32),
            pltpu.VMEM((8, BLOCKS, 64, 128), jnp.bfloat16),
            pltpu.VMEM((8, BLOCKS, 64, 128), f32),
            pltpu.VMEM((BLOCKS, 64, 128), f32),
            pltpu.VMEM((4, 8, ROWS, 128), f32),
            pltpu.VMEM((CHUNKS, 4 * CHUNK, 64, 128), i16),
            pltpu.VMEM((CHUNKS, 4 * CHUNK, 64, 128), i16),
            pltpu.VMEM((CHUNKS, 6 * CHUNK, 64, 128), i16),
            pltpu.VMEM((2, CHUNKS, 6 * CHUNK, 64, 128), i16),
            pltpu.VMEM((2, CHUNKS, 4 * CHUNK, 64, 128), i16),
            pltpu.VMEM((2, 2, 272, 128), f32),
            pltpu.VMEM((16, 8, 512), f32),
            pltpu.VMEM((528, 128), f32),
            pltpu.VMEM((17, 16, 128), i16),
            pltpu.VMEM((17, 16, 128), i16),
            pltpu.VMEM((17, 16, 128), i16),
            pltpu.VMEM((2, 17, 16, 128), i16),
            pltpu.VMEM((2, 17, 16, 128), i16),
            pltpu.VMEM((7, 4, 64, 128), f32),
            dma((10,)),
            dma((CHUNKS,)),
            dma((CHUNKS,)),
            dma((2, CHUNKS)),
            dma((2, CHUNKS)),
            dma((2, CHUNKS)),
            dma((2, CHUNKS)),
            dma,
            dma,
            dma((2,)),
            dma((2,)),
            dma((2,)),
            dma((2,)),
            dma((7,)),
            dma((7,)),
        ],
        compiler_params=pltpu.CompilerParams(
            collective_id=0, has_side_effects=True, vmem_limit_bytes=62 * 1024 * 1024
        ),
    )(*fields, speed, shape, records, *args[7:])


def solution(mesh):
    in_specs = (
        P("shot", "xy", None, None),
        P("shot", "xy", None, None),
        P("shot", "xy", None, None),
        P("shot", "xy", None, None),
        P("shot", None, "xy", None),
        P("xy", None, None),
        P("xy", None, None),
        P(),
        P(),
        P(),
        P(),
        P(),
    )
    return jax.shard_map(
        on_device, mesh=mesh, in_specs=in_specs, out_specs=P("xy", "shot", None), check_vma=False
    )
```

```python
import functools

import jax
import jax.numpy as jnp
from jax import lax
from jax.experimental import pallas as pl
from jax.experimental.pallas import tpu as pltpu
from jax.sharding import PartitionSpec as P

MESH = pl.DeviceIdType.MESH
TOP = 32767.0
BLOCKS = 33
CHUNK = 3
CHUNKS = BLOCKS // CHUNK
ROWS = 8 * BLOCKS
STEPS = 7
SENT_EARLY = 6
AHEAD = 3
WIDE = 22
FIELD_TOP = 6.0
RECORD_TOP = 12.0
SPEED_TOP = 0.25
SHAPE_TOP = 0.3
SUM_TOP = 2.0**30


def root_code(x, top):
    size = jnp.sqrt(jnp.sqrt(jnp.abs(x) * (1.0 / top))) * TOP
    size = jnp.minimum(jnp.round(size), TOP)
    return jnp.where(x < 0.0, -size, size).astype(jnp.int32).astype(jnp.int16)


def root_value(code, top):
    part = code.astype(jnp.int32).astype(jnp.float32) * (1.0 / TOP)
    return (part * part) * (part * jnp.abs(part)) * top


def long_code(x):
    size = jnp.abs(x) * (1.0 / SUM_TOP)
    for _ in range(4):
        size = jnp.sqrt(size)
    size = jnp.minimum(jnp.round(size * TOP), TOP)
    return jnp.where(x < 0.0, -size, size).astype(jnp.int32).astype(jnp.int16)


def long_value(code):
    part = code.astype(jnp.int32).astype(jnp.float32) * (1.0 / TOP)
    power = jnp.abs(part)
    for _ in range(4):
        power = power * power
    return jnp.where(part < 0.0, -power, power) * SUM_TOP


def line_code(x, top):
    return jnp.round(x * (TOP / top)).astype(jnp.int32).astype(jnp.int16)


def line_value(code, top):
    return code.astype(jnp.int32).astype(jnp.float32) * (top / TOP)


def kernel(
    fields0, fields1, fields2, fields3, speed_hbm, shape_hbm, records, wavelet, shot_x, shot_y, aperture, snap_steps,
    out,
    state, slope, speed, snap_u, snap_w, total, stage, z_out, z_in, near, near_in, far_in,
    inject, marks, turned, rec_z, rec_near, rec_z_in, rec_near_in, rec_far_in, sum_out, sums,
    in_sem, z_send, z_recv, near_send, near_recv, far_send, far_recv,
    rz_send, rz_recv, rn_send, rn_recv, rf_send, rf_recv, sum_send, sum_recv,
):
    fields = (fields0, fields1, fields2, fields3)
    s, q = lax.axis_index("shot"), lax.axis_index("xy")
    half = s // 8
    across = lax.rem(s + 8, 16)
    left, right = lax.rem(q + 15, 16), lax.rem(q + 1, 16)
    sides = ((s, left), (s, right))
    base = pl.multiple_of(248 * half, 8)
    their_base = pl.multiple_of(248 * (1 - half), 8)

    loads = []
    for f in range(4):
        loads.append(pltpu.make_async_copy(fields[f].at[0, :, pl.ds(their_base, ROWS), :], stage.at[f], in_sem.at[f]))
    for f in range(4):
        loads.append(pltpu.make_async_copy(fields[f].at[0, :, pl.ds(base, ROWS), :], state.at[f, pl.ds(7, 8), pl.ds(8, ROWS), :], in_sem.at[4 + f]))
    loads.append(pltpu.make_async_copy(shape_hbm.at[:, pl.ds(base, ROWS), :], slope.at[pl.ds(7, 8)], in_sem.at[8]))
    loads.append(pltpu.make_async_copy(speed_hbm.at[:, pl.ds(base, ROWS), :], speed.at[pl.ds(7, 8)], in_sem.at[9]))
    for load in loads[:4]:
        load.start()

    barrier = pltpu.get_barrier_semaphore()
    peers = [(across, q), *sides]
    for k in range(1, 8):
        peers.append((8 * half + lax.rem(s + k, 8), q))
    for peer in peers:
        pl.semaphore_signal(barrier, inc=1, device_id=peer, device_id_type=MESH)

    def remote(src, dst, send, recv, target):
        return pltpu.make_async_remote_copy(
            src_ref=src, dst_ref=dst, send_sem=send, recv_sem=recv, device_id=target, device_id_type=MESH
        )

    def z_copy(j):
        return remote(z_out.at[j], z_in.at[j], z_send.at[j], z_recv.at[j], (across, q))

    def near_copy(j, side):
        return remote(near.at[j], near_in.at[1 - side, j], near_send.at[side, j], near_recv.at[1 - side, j], sides[side])

    def far_copy(j, side):
        return remote(z_in.at[j], far_in.at[1 - side, j], far_send.at[side, j], far_recv.at[1 - side, j], sides[side])

    def arrived(copy_of, j, side):
        return copy_of(j, 1 - side)

    def rec_near_copy(side):
        return remote(rec_near, rec_near_in.at[1 - side], rn_send.at[side], rn_recv.at[1 - side], sides[side])

    def rec_far_copy(side):
        return remote(rec_z_in, rec_far_in.at[1 - side], rf_send.at[side], rf_recv.at[1 - side], sides[side])

    rec_z_copy = remote(rec_z, rec_z_in, rz_send, rz_recv, (across, q))

    def encode(j):
        for f in range(4):
            for i in range(CHUNK):
                row = pl.multiple_of(8 * (CHUNK * j + i), 8)
                block = stage[f, :, pl.ds(row, 8), :].reshape(64, 128)
                z_out[j, CHUNK * f + i] = root_code(block, FIELD_TOP)

    for load in loads[:4]:
        load.wait()
    for load in loads[4:]:
        load.start()
    encode(0)
    pl.semaphore_wait(barrier, len(peers))
    z_copy(0).start()

    marks[...] = jnp.zeros_like(marks)
    for t in range(STEPS):
        for x in range(8):
            marks[x, t : t + 1, :] = records[0, t, x : x + 1, :]
    turned[pl.ds(512, 16)] = jnp.zeros((16, 128), jnp.float32)
    turned[pl.ds(0, 512)] = jnp.transpose(marks[...].reshape(128, 512), (1, 0))

    @pl.loop(0, 17)
    def _(k):
        row = 16 * k
        rec_z[k] = root_code(turned[pl.ds(pl.multiple_of(their_base + row, 8), 16), :], RECORD_TOP)
        rec_near[k] = root_code(turned[pl.ds(pl.multiple_of(base + row, 8), 16), :], RECORD_TOP)

    rec_z_copy.start()
    for side in range(2):
        rec_near_copy(side).start()

    @pl.loop(1, CHUNKS)
    def _(j):
        encode(j)

        @pl.when(j < AHEAD)
        def _():
            z_copy(j).start()

    for load in loads[4:]:
        load.wait()

    @pl.loop(0, CHUNKS)
    def _(j):
        for i in range(CHUNK):
            row = pl.multiple_of(8 * (CHUNK * j + i), 8)
            for f in range(4):
                block = state[f, 7:15, pl.ds(row + 8, 8), :].reshape(64, 128)
                near[j, CHUNK * f + i] = root_code(block, FIELD_TOP)
            near[j, CHUNK * 4 + i] = line_code(slope[7:15, pl.ds(row, 8), :].reshape(64, 128), SHAPE_TOP)
            near[j, CHUNK * 5 + i] = line_code(speed[7:15, pl.ds(row, 8), :].reshape(64, 128), SPEED_TOP)
        for side in range(2):
            near_copy(j, side).start()

    lane = lax.broadcasted_iota(jnp.int32, (8, 128), 1)
    sub = lax.broadcasted_iota(jnp.int32, (8, 128), 0)
    wide_lane = lax.broadcasted_iota(jnp.int32, (16, 128), 1)
    has = (jnp.where(q > 0, 1.0, 0.0), jnp.where(q < 15, 1.0, 0.0))

    def fill_source(shot):
        tag = jnp.zeros((8, 128), jnp.float32)
        for t in range(STEPS):
            tag = jnp.where((lane & 7) == t, wavelet[t, shot], tag)
        at_x = shot_x[shot] - 8 * q + 7
        at_y = shot_y[shot] - base

        @pl.loop(0, BLOCKS)
        def _(k):
            row = pl.multiple_of(8 * k, 8)
            for g in range(2):
                hit = ((sub + row) == at_y) & (((lane >> 3) + 16 * g) == at_x)
                inject[0, g, pl.ds(row, 8), :] = jnp.where(hit, tag, 0.0)

    def fill_records(middle, beside):
        @pl.loop(0, 17)
        def _(k):
            row = pl.multiple_of(16 * k, 8)
            low = pltpu.roll(root_value(beside[0, k], RECORD_TOP), 120, 1) * has[0]
            mid = pltpu.roll(root_value(middle[k], RECORD_TOP), 56, 1)
            high = pltpu.roll(root_value(beside[1, k], RECORD_TOP), 120, 1) * has[1]
            inject[1, 0, pl.ds(row, 16), :] = jnp.where(wide_lane < 56, low, jnp.where(wide_lane < 120, mid, high))
            inject[1, 1, pl.ds(row, 16), :] = high

    for f in range(4):
        state[f, :, 0:8, :] = jnp.zeros((WIDE, 8, 128), jnp.float32)
        state[f, :, ROWS + 8 : ROWS + 16, :] = jnp.zeros((WIDE, 8, 128), jnp.float32)

    def imaged(shot):
        inside = jnp.float32(0.0)
        for i in range(8):
            inside = inside + jnp.where(aperture[i, shot] == q, 1.0, 0.0)
        scale = []
        for t in range(1, 9):
            hit = jnp.float32(0.0)
            for i in range(4):
                hit = hit + jnp.where(snap_steps[i] == t, 1.0, 0.0)
            scale.append(hit * inside)
        return scale

    own_scale, other_scale = imaged(s), imaged(across)

    def rounded(x):
        return x.astype(jnp.bfloat16).astype(jnp.float32)

    def layers(n, size):
        found = []
        for low, high in ((n, 7), (7, 15), (15, WIDE - n)):
            found += [(x, min(x + size, high)) for x in range(low, high, size)]
        return found

    def one_step(phase, n, k, blocks, size):
        tall = 8 * blocks
        row = pl.multiple_of(8 * k, 8)
        here, flat_here = pl.ds(pl.multiple_of(row + 8, 8), tall), pl.ds(row, tall)
        for x0, x1 in layers(n, size):
            count = x1 - x0
            at = lax.broadcasted_iota(jnp.int32, (count, tall, 128), 2)
            for w in range(2):
                old, now = 2 * w + (n - 1) % 2, 2 * w + n % 2
                entry = n - 1 if w == 0 else STEPS - n
                big = state[now, x0 - 1 : x1 + 1, here, :]
                mid = big[1:-1]
                lateral = big[:-2] + big[2:]
                beside = state[now, x0:x1, pl.ds(row + 7, tall), :] + state[now, x0:x1, pl.ds(row + 9, tall), :]
                lateral = lateral + beside - 4.0 * mid
                added = jnp.stack([
                    pltpu.roll(inject[w, x // 16, flat_here, :], (128 - 8 * (x % 16) - entry) % 128, 1)
                    for x in range(x0, x1)
                ])
                up = jnp.where(at == 0, added, pltpu.roll(mid, 1, 2))
                down = jnp.where(at == 127, 0.0, pltpu.roll(mid, 127, 2))
                twice = 2.0 * mid
                new = twice - state[old, x0:x1, here, :]
                new = new + slope[x0:x1, flat_here, :] * lateral + speed[x0:x1, flat_here, :] * (up + down - twice)
                state[old, x0:x1, here, :] = new
                if not 7 <= x0 < 15:
                    continue
                for i in range(blocks):
                    flat = new[:, 8 * i : 8 * i + 8, :].reshape(8 * count, 128)
                    part = pl.ds(8 * (x0 - 7), 8 * count)
                    if phase == 0 and w == 0:
                        snap_u[n, k + i, part] = flat.astype(jnp.bfloat16)
                    elif phase == 0:
                        snap_w[STEPS - n, k + i, part] = flat
                    elif w == 0:
                        total[k + i, part] += other_scale[n] * rounded(flat) * snap_w[n, k + i, part]
                    else:
                        level = STEPS - n
                        total[k + i, part] += own_scale[level] * flat * snap_u[level, k + i, part].astype(jnp.float32)

    def spread(f, rows, low, high, mid=None):
        state[f, 0:7, rows, :] = (root_value(low, FIELD_TOP) * has[0]).reshape(8, 8, 128)[1:8]
        state[f, 15:22, rows, :] = (root_value(high, FIELD_TOP) * has[1]).reshape(8, 8, 128)[0:7]
        if mid is not None:
            mid = root_value(mid, FIELD_TOP)
            state[f, 7:15, rows, :] = mid.reshape(8, 8, 128)
        return mid

    def open_near(j):
        @pl.loop(0, CHUNK)
        def _(i):
            k = CHUNK * j + i
            row = pl.multiple_of(8 * k, 8)
            rows = pl.ds(pl.multiple_of(row + 8, 8), 8)
            for f in range(4):
                spread(f, rows, near_in[0, j, CHUNK * f + i], near_in[1, j, CHUNK * f + i])
            snap_u[0, k] = state[1, 7:15, rows, :].reshape(64, 128).astype(jnp.bfloat16)
            snap_w[STEPS, k] = state[3, 7:15, rows, :].reshape(64, 128)
            for side, cut, into in ((0, slice(1, 8), slice(0, 7)), (1, slice(0, 7), slice(15, 22))):
                tilt = line_value(near_in[side, j, CHUNK * 4 + i], SHAPE_TOP)
                fast = line_value(near_in[side, j, CHUNK * 5 + i], SPEED_TOP) * has[side]
                speed[into, pl.ds(row, 8), :] = fast.reshape(8, 8, 128)[cut]
                slope[into, pl.ds(row, 8), :] = (fast * (1.0 + 2.0 * tilt)).reshape(8, 8, 128)[cut]
            fast = speed[7:15, pl.ds(row, 8), :]
            slope[7:15, pl.ds(row, 8), :] = fast * (1.0 + 2.0 * slope[7:15, pl.ds(row, 8), :])

    def open_far(j):
        @pl.loop(0, CHUNK)
        def _(i):
            k = CHUNK * j + i
            rows = pl.ds(pl.multiple_of(8 * k + 8, 8), 8)
            mids = []
            for f in range(4):
                at = CHUNK * f + i
                mids.append(spread(f, rows, far_in[0, j, at], far_in[1, j, at], z_in[j, at]))
            total[k] = (
                other_scale[0] * rounded(mids[1]) * snap_w[0, k]
                + own_scale[STEPS] * mids[3] * snap_u[STEPS, k].astype(jnp.float32)
            )

    def advance(phase, j):
        for n in range(1, STEPS + 1):
            first = jnp.maximum(CHUNK * j - n, 0)
            last = jnp.where(j == CHUNKS - 1, BLOCKS, jnp.maximum(CHUNK * j + CHUNK - n, 0))
            threes = (last - first) // CHUNK

            @pl.loop(0, threes)
            def _(i):
                one_step(phase, n, first + CHUNK * i, CHUNK, 4)

            @pl.loop(first + CHUNK * threes, last)
            def _(k):
                one_step(phase, n, k, 1, 8)

    mine = lax.rem(s, 8)

    def sum_copy(k):
        part = lax.rem(s + k, 8)
        return remote(sum_out.at[part], sums.at[k - 1], sum_send.at[k - 1], sum_recv.at[k - 1], (8 * half + part, q))

    def send_sums(part):
        @pl.when(part != mine)
        def _():
            for i in range(4):
                sum_out[part, i] = long_code(total[half + 4 * part + i])
            sum_copy(lax.rem(part - mine + 8, 8)).start()

    fill_source(s)
    for side in range(2):
        rec_near_copy(1 - side).wait_recv()
    fill_records(rec_near, rec_near_in)

    @pl.loop(0, CHUNKS)
    def _(j):
        for side in range(2):
            near_copy(j, 1 - side).wait_recv()
        open_near(j)
        advance(0, j)

        @pl.when((lax.rem(j, 3) == 2) & (j // 3 + AHEAD < SENT_EARLY))
        def _():
            z_copy(j // 3).wait_send()
            z_copy(j // 3 + AHEAD).start()

    rec_z_copy.wait_recv()
    for side in range(2):
        rec_far_copy(side).start()
    fill_source(across)
    for side in range(2):
        rec_far_copy(1 - side).wait_recv()
    fill_records(rec_z_in, rec_far_in)

    @pl.loop(0, CHUNKS + 1)
    def _(j):
        @pl.when(j < CHUNKS)
        def _():
            z_copy(j).wait_recv()
            for side in range(2):
                far_copy(j, side).start()

        @pl.when((j >= SENT_EARLY - 2) & (j < CHUNKS - 2))
        def _():
            z_copy(j).wait_send()
            z_copy(j + 2).start()

        @pl.when(j > 0)
        def _():
            for side in range(2):
                far_copy(j - 1, 1 - side).wait_recv()
            open_far(j - 1)
            advance(1, j - 1)
        for part, ready in ((0, 5), (2, 7)):
            @pl.when(j - 1 == ready)
            def _():
                send_sums(part)
                send_sums(part + 1)

    for part in range(4, 8):
        send_sums(part)
    for k in range(1, 8):
        sum_copy(k).wait_recv()
    for i in range(4):
        value = total[half + 4 * mine + i]
        for k in range(7):
            value = value + long_value(sums[k, i])
        out[:, 8 * i : 8 * i + 8, :] = value.reshape(8, 8, 128)

    @pl.loop(0, CHUNKS)
    def _(j):
        @pl.when(((j >= SENT_EARLY - AHEAD) & (j < SENT_EARLY - 2)) | (j >= CHUNKS - 2))
        def _():
            z_copy(j).wait_send()
        for side in range(2):
            near_copy(j, side).wait_send()
            far_copy(j, side).wait_send()

    rec_z_copy.wait_send()
    for side in range(2):
        rec_near_copy(side).wait_send()
        rec_far_copy(side).wait_send()
    for k in range(1, 8):
        sum_copy(k).wait_send()


def on_device(*args):
    f32, i16 = jnp.float32, jnp.int16
    dma = pltpu.SemaphoreType.DMA
    fields = (args[0], args[1], args[2], args[3])
    records, speed, shape = args[4], args[5], args[6]
    anywhere, smem = pl.BlockSpec(memory_space=pl.ANY), pl.BlockSpec(memory_space=pltpu.SMEM)
    vmem = pl.BlockSpec(memory_space=pltpu.VMEM)
    return pl.pallas_call(
        kernel,
        out_shape=jax.ShapeDtypeStruct((8, 32, 128), f32),
        in_specs=[anywhere] * 6 + [vmem] + [smem] * 5,
        out_specs=vmem,
        scratch_shapes=[
            pltpu.VMEM((4, WIDE, ROWS + 16, 128), f32),
            pltpu.VMEM((WIDE, ROWS, 128), f32),
            pltpu.VMEM((WIDE, ROWS, 128), f32),
            pltpu.VMEM((8, BLOCKS, 64, 128), jnp.bfloat16),
            pltpu.VMEM((8, BLOCKS, 64, 128), f32),
            pltpu.VMEM((BLOCKS, 64, 128), f32),
            pltpu.VMEM((4, 8, ROWS, 128), f32),
            pltpu.VMEM((CHUNKS, 4 * CHUNK, 64, 128), i16),
            pltpu.VMEM((CHUNKS, 4 * CHUNK, 64, 128), i16),
            pltpu.VMEM((CHUNKS, 6 * CHUNK, 64, 128), i16),
            pltpu.VMEM((2, CHUNKS, 6 * CHUNK, 64, 128), i16),
            pltpu.VMEM((2, CHUNKS, 4 * CHUNK, 64, 128), i16),
            pltpu.VMEM((2, 2, 272, 128), f32),
            pltpu.VMEM((16, 8, 512), f32),
            pltpu.VMEM((528, 128), f32),
            pltpu.VMEM((17, 16, 128), i16),
            pltpu.VMEM((17, 16, 128), i16),
            pltpu.VMEM((17, 16, 128), i16),
            pltpu.VMEM((2, 17, 16, 128), i16),
            pltpu.VMEM((2, 17, 16, 128), i16),
            pltpu.VMEM((8, 4, 64, 128), i16),
            pltpu.VMEM((7, 4, 64, 128), i16),
            dma((10,)),
            dma((CHUNKS,)),
            dma((CHUNKS,)),
            dma((2, CHUNKS)),
            dma((2, CHUNKS)),
            dma((2, CHUNKS)),
            dma((2, CHUNKS)),
            dma,
            dma,
            dma((2,)),
            dma((2,)),
            dma((2,)),
            dma((2,)),
            dma((7,)),
            dma((7,)),
        ],
        compiler_params=pltpu.CompilerParams(
            collective_id=0, has_side_effects=True, vmem_limit_bytes=62 * 1024 * 1024
        ),
    )(*fields, speed, shape, records, args[7].T, args[8], args[9], args[10].T, args[11])


def solution(mesh):
    in_specs = (
        P("shot", "xy", None, None),
        P("shot", "xy", None, None),
        P("shot", "xy", None, None),
        P("shot", "xy", None, None),
        P("shot", None, "xy", None),
        P("xy", None, None),
        P("xy", None, None),
        P(),
        P(),
        P(),
        P(),
        P(),
    )
    return jax.shard_map(
        on_device, mesh=mesh, in_specs=in_specs, out_specs=P("xy", "shot", None), check_vma=False
    )
```

```python
import functools

import jax
import jax.numpy as jnp
from jax import lax
from jax.experimental import pallas as pl
from jax.experimental.pallas import tpu as pltpu
from jax.sharding import PartitionSpec as P

MESH = pl.DeviceIdType.MESH
TOP = 32767.0
BLOCKS = 33
CHUNK = 3
CHUNKS = BLOCKS // CHUNK
ROWS = 8 * BLOCKS
STEPS = 7
BESIDE = 5
SENT_EARLY = 8
AHEAD = 5
WIDE = 22
FIELD_TOP = 6.0
RECORD_TOP = 12.0
SPEED_TOP = 0.25
SHAPE_TOP = 0.3
SUM_TOP = 2.0**30


def root_code(x, top):
    size = jnp.sqrt(jnp.sqrt(jnp.abs(x) * (1.0 / top))) * TOP
    size = jnp.minimum(jnp.round(size), TOP)
    return jnp.where(x < 0.0, -size, size).astype(jnp.int32).astype(jnp.int16)


def root_value(code, top):
    part = code.astype(jnp.int32).astype(jnp.float32) * (1.0 / TOP)
    return (part * part) * (part * jnp.abs(part)) * top


def long_code(x):
    size = jnp.abs(x) * (1.0 / SUM_TOP)
    for _ in range(4):
        size = jnp.sqrt(size)
    size = jnp.minimum(jnp.round(size * TOP), TOP)
    return jnp.where(x < 0.0, -size, size).astype(jnp.int32).astype(jnp.int16)


def long_value(code):
    part = code.astype(jnp.int32).astype(jnp.float32) * (1.0 / TOP)
    power = jnp.abs(part)
    for _ in range(4):
        power = power * power
    return jnp.where(part < 0.0, -power, power) * SUM_TOP


def line_code(x, top):
    return jnp.round(x * (TOP / top)).astype(jnp.int32).astype(jnp.int16)


def line_value(code, top):
    return code.astype(jnp.int32).astype(jnp.float32) * (top / TOP)


def kernel(
    fields0, fields1, fields2, fields3, speed_hbm, shape_hbm, records, wavelet, shot_x, shot_y, aperture, snap_steps,
    out,
    state, slope, speed, snap_u, snap_w, total, stage, z_out, z_in, near, near_in, far_in,
    inject, marks, turned, rec_z, rec_near, rec_z_in, rec_near_in, rec_far_in, sum_out, sums,
    in_sem, z_send, z_recv, near_send, near_recv, far_send, far_recv,
    rz_send, rz_recv, rn_send, rn_recv, rf_send, rf_recv, sum_send, sum_recv,
):
    fields = (fields0, fields1, fields2, fields3)
    s, q = lax.axis_index("shot"), lax.axis_index("xy")
    half = s // 8
    across = lax.rem(s + 8, 16)
    left, right = lax.rem(q + 15, 16), lax.rem(q + 1, 16)
    sides = ((s, left), (s, right))
    base = pl.multiple_of(248 * half, 8)
    their_base = pl.multiple_of(248 * (1 - half), 8)

    firsts, loads = [], []
    tall = 8 * CHUNK
    for f in range(4):
        theirs = fields[f].at[0]
        rest = pl.ds(pl.multiple_of(their_base + tall, 8), ROWS - tall)
        firsts.append(pltpu.make_async_copy(theirs.at[:, pl.ds(their_base, tall), :], stage.at[f, :, pl.ds(0, tall), :], in_sem.at[10 + f]))
        loads.append(pltpu.make_async_copy(theirs.at[:, rest, :], stage.at[f, :, pl.ds(tall, ROWS - tall), :], in_sem.at[f]))
    for f in range(4):
        loads.append(pltpu.make_async_copy(fields[f].at[0, :, pl.ds(base, ROWS), :], state.at[f, pl.ds(7, 8), pl.ds(8, ROWS), :], in_sem.at[4 + f]))
    loads.append(pltpu.make_async_copy(shape_hbm.at[:, pl.ds(base, ROWS), :], slope.at[pl.ds(7, 8)], in_sem.at[8]))
    loads.append(pltpu.make_async_copy(speed_hbm.at[:, pl.ds(base, ROWS), :], speed.at[pl.ds(7, 8)], in_sem.at[9]))
    for load in firsts + loads[:4]:
        load.start()

    barrier = pltpu.get_barrier_semaphore()
    peers = [(across, q), *sides]
    for k in range(1, 8):
        peers.append((8 * half + lax.rem(s + k, 8), q))
    for peer in peers:
        pl.semaphore_signal(barrier, inc=1, device_id=peer, device_id_type=MESH)

    def remote(src, dst, send, recv, target):
        return pltpu.make_async_remote_copy(
            src_ref=src, dst_ref=dst, send_sem=send, recv_sem=recv, device_id=target, device_id_type=MESH
        )

    def z_copy(j):
        return remote(z_out.at[j], z_in.at[j], z_send.at[j], z_recv.at[j], (across, q))

    def near_copy(j, side):
        return remote(near.at[j], near_in.at[1 - side, j], near_send.at[side, j], near_recv.at[1 - side, j], sides[side])

    def far_copy(j, side):
        return remote(z_in.at[j], far_in.at[1 - side, j], far_send.at[side, j], far_recv.at[1 - side, j], sides[side])

    def arrived(copy_of, j, side):
        return copy_of(j, 1 - side)

    def rec_near_copy(side):
        return remote(rec_near, rec_near_in.at[1 - side], rn_send.at[side], rn_recv.at[1 - side], sides[side])

    def rec_far_copy(side):
        return remote(rec_z_in, rec_far_in.at[1 - side], rf_send.at[side], rf_recv.at[1 - side], sides[side])

    rec_z_copy = remote(rec_z, rec_z_in, rz_send, rz_recv, (across, q))

    def encode(j):
        for f in range(4):
            for i in range(CHUNK):
                row = pl.multiple_of(8 * (CHUNK * j + i), 8)
                block = stage[f, :, pl.ds(row, 8), :].reshape(64, 128)
                z_out[j, CHUNK * f + i] = root_code(block, FIELD_TOP)

    for load in firsts:
        load.wait()
    for load in loads[4:]:
        load.start()
    encode(0)
    pl.semaphore_wait(barrier, len(peers))
    z_copy(0).start()

    marks[...] = jnp.zeros_like(marks)
    for t in range(STEPS):
        for x in range(8):
            marks[x, t : t + 1, :] = records[0, t, x : x + 1, :]
    turned[pl.ds(512, 16)] = jnp.zeros((16, 128), jnp.float32)
    turned[pl.ds(0, 512)] = jnp.transpose(marks[...].reshape(128, 512), (1, 0))

    @pl.loop(0, 17)
    def _(k):
        row = 16 * k
        rec_z[k] = root_code(turned[pl.ds(pl.multiple_of(their_base + row, 8), 16), :], RECORD_TOP)
        rec_near[k] = root_code(turned[pl.ds(pl.multiple_of(base + row, 8), 16), :], RECORD_TOP)

    rec_z_copy.start()
    for side in range(2):
        rec_near_copy(side).start()

    for load in loads[:4]:
        load.wait()

    @pl.loop(1, CHUNKS)
    def _(j):
        encode(j)

        @pl.when(j < AHEAD)
        def _():
            z_copy(j).start()

    for load in loads[4:]:
        load.wait()

    @pl.loop(0, CHUNKS)
    def _(j):
        for i in range(CHUNK):
            row = pl.multiple_of(8 * (CHUNK * j + i), 8)
            for f in range(4):
                block = state[f, 7:15, pl.ds(row + 8, 8), :].reshape(64, 128)
                near[j, CHUNK * f + i] = root_code(block, FIELD_TOP)
            near[j, CHUNK * 4 + i] = line_code(slope[7:15, pl.ds(row, 8), :].reshape(64, 128), SHAPE_TOP)
            near[j, CHUNK * 5 + i] = line_code(speed[7:15, pl.ds(row, 8), :].reshape(64, 128), SPEED_TOP)
        for side in range(2):
            near_copy(j, side).start()

    lane = lax.broadcasted_iota(jnp.int32, (8, 128), 1)
    sub = lax.broadcasted_iota(jnp.int32, (8, 128), 0)
    wide_lane = lax.broadcasted_iota(jnp.int32, (16, 128), 1)
    has = (jnp.where(q > 0, 1.0, 0.0), jnp.where(q < 15, 1.0, 0.0))

    def fill_source(shot):
        tag = jnp.zeros((8, 128), jnp.float32)
        for t in range(STEPS):
            tag = jnp.where((lane & 7) == t, wavelet[t, shot], tag)
        at_x = shot_x[shot] - 8 * q + 7
        at_y = shot_y[shot] - base

        @pl.loop(0, BLOCKS)
        def _(k):
            row = pl.multiple_of(8 * k, 8)
            for g in range(2):
                hit = ((sub + row) == at_y) & (((lane >> 3) + 16 * g) == at_x)
                inject[0, g, pl.ds(row, 8), :] = jnp.where(hit, tag, 0.0)

    def fill_records(middle, beside):
        @pl.loop(0, 17)
        def _(k):
            row = pl.multiple_of(16 * k, 8)
            low = pltpu.roll(root_value(beside[0, k], RECORD_TOP), 120, 1) * has[0]
            mid = pltpu.roll(root_value(middle[k], RECORD_TOP), 56, 1)
            high = pltpu.roll(root_value(beside[1, k], RECORD_TOP), 120, 1) * has[1]
            inject[1, 0, pl.ds(row, 16), :] = jnp.where(wide_lane < 56, low, jnp.where(wide_lane < 120, mid, high))
            inject[1, 1, pl.ds(row, 16), :] = high

    for f in range(4):
        state[f, :, 0:8, :] = jnp.zeros((WIDE, 8, 128), jnp.float32)
        state[f, :, ROWS + 8 : ROWS + 16, :] = jnp.zeros((WIDE, 8, 128), jnp.float32)

    def imaged(shot):
        inside = jnp.float32(0.0)
        for i in range(8):
            inside = inside + jnp.where(aperture[i, shot] == q, 1.0, 0.0)
        scale = []
        for t in range(1, 9):
            hit = jnp.float32(0.0)
            for i in range(4):
                hit = hit + jnp.where(snap_steps[i] == t, 1.0, 0.0)
            scale.append(hit * inside)
        return scale

    own_scale, other_scale = imaged(s), imaged(across)

    def rounded(x):
        return x.astype(jnp.bfloat16).astype(jnp.float32)

    def layers(n, size):
        found = []
        for low, high in ((n, 7), (7, 15), (15, WIDE - n)):
            found += [(x, min(x + size, high)) for x in range(low, high, size)]
        return found

    def one_step(phase, n, k, blocks, size):
        tall = 8 * blocks
        row = pl.multiple_of(8 * k, 8)
        here, flat_here = pl.ds(pl.multiple_of(row + 8, 8), tall), pl.ds(row, tall)
        for x0, x1 in layers(n, size):
            count = x1 - x0
            at = lax.broadcasted_iota(jnp.int32, (count, tall, 128), 2)
            for w in range(2):
                old, now = 2 * w + (n - 1) % 2, 2 * w + n % 2
                entry = n - 1 if w == 0 else STEPS - n
                big = state[now, x0 - 1 : x1 + 1, here, :]
                mid = big[1:-1]
                lateral = big[:-2] + big[2:]
                beside = state[now, x0:x1, pl.ds(row + 7, tall), :] + state[now, x0:x1, pl.ds(row + 9, tall), :]
                lateral = lateral + beside - 4.0 * mid
                added = jnp.stack([
                    pltpu.roll(inject[w, x // 16, flat_here, :], (128 - 8 * (x % 16) - entry) % 128, 1)
                    for x in range(x0, x1)
                ])
                up = jnp.where(at == 0, added, pltpu.roll(mid, 1, 2))
                down = jnp.where(at == 127, 0.0, pltpu.roll(mid, 127, 2))
                twice = 2.0 * mid
                new = twice - state[old, x0:x1, here, :]
                new = new + slope[x0:x1, flat_here, :] * lateral + speed[x0:x1, flat_here, :] * (up + down - twice)
                state[old, x0:x1, here, :] = new
                if not 7 <= x0 < 15:
                    continue
                for i in range(blocks):
                    flat = new[:, 8 * i : 8 * i + 8, :].reshape(8 * count, 128)
                    part = pl.ds(8 * (x0 - 7), 8 * count)
                    if phase == 0 and w == 0:
                        snap_u[n, k + i, part] = flat.astype(jnp.bfloat16)
                    elif phase == 0:
                        snap_w[STEPS - n, k + i, part] = flat
                    elif w == 0:
                        total[k + i, part] += other_scale[n] * rounded(flat) * snap_w[n, k + i, part]
                    else:
                        level = STEPS - n
                        total[k + i, part] += own_scale[level] * flat * snap_u[level, k + i, part].astype(jnp.float32)

    def spread(f, rows, low, high, mid=None):
        state[f, 0:7, rows, :] = (root_value(low, FIELD_TOP) * has[0]).reshape(8, 8, 128)[1:8]
        state[f, 15:22, rows, :] = (root_value(high, FIELD_TOP) * has[1]).reshape(8, 8, 128)[0:7]
        if mid is not None:
            mid = root_value(mid, FIELD_TOP)
            state[f, 7:15, rows, :] = mid.reshape(8, 8, 128)
        return mid

    def open_near(j):
        @pl.loop(0, CHUNK)
        def _(i):
            k = CHUNK * j + i
            row = pl.multiple_of(8 * k, 8)
            rows = pl.ds(pl.multiple_of(row + 8, 8), 8)
            for f in range(4):
                spread(f, rows, near_in[0, j, CHUNK * f + i], near_in[1, j, CHUNK * f + i])
            snap_u[0, k] = state[1, 7:15, rows, :].reshape(64, 128).astype(jnp.bfloat16)
            snap_w[STEPS, k] = state[3, 7:15, rows, :].reshape(64, 128)
            for side, cut, into in ((0, slice(1, 8), slice(0, 7)), (1, slice(0, 7), slice(15, 22))):
                tilt = line_value(near_in[side, j, CHUNK * 4 + i], SHAPE_TOP)
                fast = line_value(near_in[side, j, CHUNK * 5 + i], SPEED_TOP) * has[side]
                speed[into, pl.ds(row, 8), :] = fast.reshape(8, 8, 128)[cut]
                slope[into, pl.ds(row, 8), :] = (fast * (1.0 + 2.0 * tilt)).reshape(8, 8, 128)[cut]
            fast = speed[7:15, pl.ds(row, 8), :]
            slope[7:15, pl.ds(row, 8), :] = fast * (1.0 + 2.0 * slope[7:15, pl.ds(row, 8), :])

    def open_far(j):
        @pl.loop(0, CHUNK)
        def _(i):
            k = CHUNK * j + i
            rows = pl.ds(pl.multiple_of(8 * k + 8, 8), 8)
            mids = []
            for f in range(4):
                at = CHUNK * f + i
                mids.append(spread(f, rows, far_in[0, j, at], far_in[1, j, at], z_in[j, at]))
            total[k] = (
                other_scale[0] * rounded(mids[1]) * snap_w[0, k]
                + own_scale[STEPS] * mids[3] * snap_u[STEPS, k].astype(jnp.float32)
            )

    def advance(phase, j):
        for n in range(1, STEPS + 1):
            first = jnp.maximum(CHUNK * j - n, 0)
            last = jnp.where(j == CHUNKS - 1, BLOCKS, jnp.maximum(CHUNK * j + CHUNK - n, 0))
            threes = (last - first) // CHUNK

            @pl.loop(0, threes)
            def _(i):
                one_step(phase, n, first + CHUNK * i, CHUNK, 4)

            @pl.loop(first + CHUNK * threes, last)
            def _(k):
                one_step(phase, n, k, 1, 8)

    mine = lax.rem(s, 8)

    def sum_copy(k):
        part = lax.rem(s + k, 8)
        return remote(sum_out.at[part], sums.at[k - 1], sum_send.at[k - 1], sum_recv.at[k - 1], (8 * half + part, q))

    def send_sums(k):
        part = lax.rem(s + k, 8)
        for i in range(4):
            sum_out[part, i] = long_code(total[half + 4 * part + i])
        sum_copy(k).start()

    fill_source(s)
    for side in range(2):
        rec_near_copy(1 - side).wait_recv()
    fill_records(rec_near, rec_near_in)

    @pl.loop(0, CHUNKS)
    def _(j):
        for side in range(2):
            near_copy(j, 1 - side).wait_recv()
        open_near(j)
        advance(0, j)

        @pl.when((lax.rem(j, 3) == 2) & (j // 3 + AHEAD < SENT_EARLY))
        def _():
            z_copy(j // 3).wait_send()
            z_copy(j // 3 + AHEAD).start()

    rec_z_copy.wait_recv()
    for side in range(2):
        rec_far_copy(side).start()

    def pass_on(j):
        z_copy(j).wait_recv()
        for side in range(2):
            far_copy(j, side).start()

    @pl.loop(0, BESIDE)
    def _(j):
        pass_on(j)

    fill_source(across)
    for side in range(2):
        rec_far_copy(1 - side).wait_recv()
    fill_records(rec_z_in, rec_far_in)

    @pl.loop(0, CHUNKS + 1)
    def _(j):
        @pl.when((j >= BESIDE) & (j < CHUNKS))
        def _():
            pass_on(j)

        @pl.when((j >= SENT_EARLY - 2) & (j < CHUNKS - 2))
        def _():
            z_copy(j).wait_send()
            z_copy(j + 2).start()

        @pl.when(j > 0)
        def _():
            for side in range(2):
                far_copy(j - 1, 1 - side).wait_recv()
            open_far(j - 1)
            advance(1, j - 1)

    for k in (4, 3, 5, 2, 6, 1, 7):
        send_sums(k)
    for k in (1, 7, 2, 6, 3, 5, 4):
        sum_copy(k).wait_recv()
        for i in range(4):
            total[half + 4 * mine + i] += long_value(sums[k - 1, i])
    for i in range(4):
        out[:, 8 * i : 8 * i + 8, :] = total[half + 4 * mine + i].reshape(8, 8, 128)

    @pl.loop(0, CHUNKS)
    def _(j):
        @pl.when(((j >= SENT_EARLY - AHEAD) & (j < SENT_EARLY - 2)) | (j >= CHUNKS - 2))
        def _():
            z_copy(j).wait_send()
        for side in range(2):
            near_copy(j, side).wait_send()
            far_copy(j, side).wait_send()

    rec_z_copy.wait_send()
    for side in range(2):
        rec_near_copy(side).wait_send()
        rec_far_copy(side).wait_send()
    for k in range(1, 8):
        sum_copy(k).wait_send()


def on_device(*args):
    f32, i16 = jnp.float32, jnp.int16
    dma = pltpu.SemaphoreType.DMA
    fields = (args[0], args[1], args[2], args[3])
    records, speed, shape = args[4], args[5], args[6]
    anywhere, smem = pl.BlockSpec(memory_space=pl.ANY), pl.BlockSpec(memory_space=pltpu.SMEM)
    vmem = pl.BlockSpec(memory_space=pltpu.VMEM)
    return pl.pallas_call(
        kernel,
        out_shape=jax.ShapeDtypeStruct((8, 32, 128), f32),
        in_specs=[anywhere] * 6 + [vmem] + [smem] * 5,
        out_specs=vmem,
        scratch_shapes=[
            pltpu.VMEM((4, WIDE, ROWS + 16, 128), f32),
            pltpu.VMEM((WIDE, ROWS, 128), f32),
            pltpu.VMEM((WIDE, ROWS, 128), f32),
            pltpu.VMEM((8, BLOCKS, 64, 128), jnp.bfloat16),
            pltpu.VMEM((8, BLOCKS, 64, 128), f32),
            pltpu.VMEM((BLOCKS, 64, 128), f32),
            pltpu.VMEM((4, 8, ROWS, 128), f32),
            pltpu.VMEM((CHUNKS, 4 * CHUNK, 64, 128), i16),
            pltpu.VMEM((CHUNKS, 4 * CHUNK, 64, 128), i16),
            pltpu.VMEM((CHUNKS, 6 * CHUNK, 64, 128), i16),
            pltpu.VMEM((2, CHUNKS, 6 * CHUNK, 64, 128), i16),
            pltpu.VMEM((2, CHUNKS, 4 * CHUNK, 64, 128), i16),
            pltpu.VMEM((2, 2, 272, 128), f32),
            pltpu.VMEM((16, 8, 512), f32),
            pltpu.VMEM((528, 128), f32),
            pltpu.VMEM((17, 16, 128), i16),
            pltpu.VMEM((17, 16, 128), i16),
            pltpu.VMEM((17, 16, 128), i16),
            pltpu.VMEM((2, 17, 16, 128), i16),
            pltpu.VMEM((2, 17, 16, 128), i16),
            pltpu.VMEM((8, 4, 64, 128), i16),
            pltpu.VMEM((7, 4, 64, 128), i16),
            dma((14,)),
            dma((CHUNKS,)),
            dma((CHUNKS,)),
            dma((2, CHUNKS)),
            dma((2, CHUNKS)),
            dma((2, CHUNKS)),
            dma((2, CHUNKS)),
            dma,
            dma,
            dma((2,)),
            dma((2,)),
            dma((2,)),
            dma((2,)),
            dma((7,)),
            dma((7,)),
        ],
        compiler_params=pltpu.CompilerParams(
            collective_id=0, has_side_effects=True, vmem_limit_bytes=62 * 1024 * 1024
        ),
    )(*fields, speed, shape, records, args[7].T, args[8], args[9], args[10].T, args[11])


def solution(mesh):
    in_specs = (
        P("shot", "xy", None, None),
        P("shot", "xy", None, None),
        P("shot", "xy", None, None),
        P("shot", "xy", None, None),
        P("shot", None, "xy", None),
        P("xy", None, None),
        P("xy", None, None),
        P(),
        P(),
        P(),
        P(),
        P(),
    )
    return jax.shard_map(
        on_device, mesh=mesh, in_specs=in_specs, out_specs=P("xy", "shot", None), check_vma=False
    )
```

```python
import functools

import jax
import jax.numpy as jnp
from jax import lax
from jax.experimental import pallas as pl
from jax.experimental.pallas import tpu as pltpu
from jax.sharding import PartitionSpec as P

MESH = pl.DeviceIdType.MESH
TOP = 32767.0
BLOCKS = 33
CHUNK = 3
CHUNKS = BLOCKS // CHUNK
ROWS = 8 * BLOCKS
STEPS = 7
BESIDE = 5
SENT_EARLY = 8
AHEAD = 5
WIDE = 22
FIELD_TOP = 6.0
RECORD_TOP = 12.0
SPEED_TOP = 0.25
SHAPE_TOP = 0.3
SUM_TOP = 2.0**30


def root_code(x, top):
    size = jnp.sqrt(jnp.sqrt(jnp.abs(x) * (1.0 / top))) * TOP
    size = jnp.minimum(jnp.round(size), TOP)
    return jnp.where(x < 0.0, -size, size).astype(jnp.int32).astype(jnp.int16)


def root_value(code, top):
    part = code.astype(jnp.int32).astype(jnp.float32) * (1.0 / TOP)
    return (part * part) * (part * jnp.abs(part)) * top


def long_code(x):
    size = jnp.abs(x) * (1.0 / SUM_TOP)
    for _ in range(4):
        size = jnp.sqrt(size)
    size = jnp.minimum(jnp.round(size * TOP), TOP)
    return jnp.where(x < 0.0, -size, size).astype(jnp.int32).astype(jnp.int16)


def long_value(code):
    part = code.astype(jnp.int32).astype(jnp.float32) * (1.0 / TOP)
    power = jnp.abs(part)
    for _ in range(4):
        power = power * power
    return jnp.where(part < 0.0, -power, power) * SUM_TOP


def line_code(x, top):
    return jnp.round(x * (TOP / top)).astype(jnp.int32).astype(jnp.int16)


def line_value(code, top):
    return code.astype(jnp.int32).astype(jnp.float32) * (top / TOP)


def kernel(
    fields0, fields1, fields2, fields3, speed_hbm, shape_hbm, records, wavelet, shot_x, shot_y, aperture, snap_steps,
    out,
    state, slope, speed, snap_u, snap_w, total, stage, z_out, z_in, near, near_in, far_in,
    inject, marks, turned, rec_z, rec_near, rec_z_in, rec_near_in, rec_far_in, sum_out, sums,
    in_sem, z_send, z_recv, near_send, near_recv, far_send, far_recv,
    rz_send, rz_recv, rn_send, rn_recv, rf_send, rf_recv, sum_send, sum_recv,
):
    fields = (fields0, fields1, fields2, fields3)
    s, q = lax.axis_index("shot"), lax.axis_index("xy")
    half = s // 8
    across = lax.rem(s + 8, 16)
    left, right = lax.rem(q + 15, 16), lax.rem(q + 1, 16)
    sides = ((s, left), (s, right))
    base = pl.multiple_of(248 * half, 8)
    their_base = pl.multiple_of(248 * (1 - half), 8)

    firsts, loads = [], []
    tall = 8 * CHUNK
    for f in range(4):
        theirs = fields[f].at[0]
        rest = pl.ds(pl.multiple_of(their_base + tall, 8), ROWS - tall)
        firsts.append(pltpu.make_async_copy(theirs.at[:, pl.ds(their_base, tall), :], stage.at[f, :, pl.ds(0, tall), :], in_sem.at[10 + f]))
        loads.append(pltpu.make_async_copy(theirs.at[:, rest, :], stage.at[f, :, pl.ds(tall, ROWS - tall), :], in_sem.at[f]))
    for f in range(4):
        loads.append(pltpu.make_async_copy(fields[f].at[0, :, pl.ds(base, ROWS), :], state.at[f, pl.ds(7, 8), pl.ds(8, ROWS), :], in_sem.at[4 + f]))
    loads.append(pltpu.make_async_copy(shape_hbm.at[:, pl.ds(base, ROWS), :], slope.at[pl.ds(7, 8)], in_sem.at[8]))
    loads.append(pltpu.make_async_copy(speed_hbm.at[:, pl.ds(base, ROWS), :], speed.at[pl.ds(7, 8)], in_sem.at[9]))
    for load in firsts + loads[:4]:
        load.start()

    barrier = pltpu.get_barrier_semaphore()
    peers = [(across, q), *sides]
    for k in range(1, 8):
        peers.append((8 * half + lax.rem(s + k, 8), q))
    for peer in peers:
        pl.semaphore_signal(barrier, inc=1, device_id=peer, device_id_type=MESH)

    def remote(src, dst, send, recv, target):
        return pltpu.make_async_remote_copy(
            src_ref=src, dst_ref=dst, send_sem=send, recv_sem=recv, device_id=target, device_id_type=MESH
        )

    def z_copy(j):
        return remote(z_out.at[j], z_in.at[j], z_send.at[j], z_recv.at[j], (across, q))

    def near_copy(j, side):
        return remote(near.at[j], near_in.at[1 - side, j], near_send.at[side, j], near_recv.at[1 - side, j], sides[side])

    def far_copy(j, side):
        return remote(z_in.at[j], far_in.at[1 - side, j], far_send.at[side, j], far_recv.at[1 - side, j], sides[side])

    def arrived(copy_of, j, side):
        return copy_of(j, 1 - side)

    def rec_near_copy(side):
        return remote(rec_near, rec_near_in.at[1 - side], rn_send.at[side], rn_recv.at[1 - side], sides[side])

    def rec_far_copy(side):
        return remote(rec_z_in, rec_far_in.at[1 - side], rf_send.at[side], rf_recv.at[1 - side], sides[side])

    rec_z_copy = remote(rec_z, rec_z_in, rz_send, rz_recv, (across, q))

    def encode(j):
        for f in range(4):
            for i in range(CHUNK):
                row = pl.multiple_of(8 * (CHUNK * j + i), 8)
                block = stage[f, :, pl.ds(row, 8), :].reshape(64, 128)
                z_out[j, CHUNK * f + i] = root_code(block, FIELD_TOP)

    for load in firsts:
        load.wait()
    for load in loads[4:]:
        load.start()
    encode(0)
    pl.semaphore_wait(barrier, len(peers))
    z_copy(0).start()

    marks[...] = jnp.zeros_like(marks)
    for t in range(STEPS):
        for x in range(8):
            marks[x, t : t + 1, :] = records[0, t, x : x + 1, :]
    turned[pl.ds(512, 16)] = jnp.zeros((16, 128), jnp.float32)
    turned[pl.ds(0, 512)] = jnp.transpose(marks[...].reshape(128, 512), (1, 0))

    @pl.loop(0, 17)
    def _(k):
        row = 16 * k
        rec_near[k] = root_code(turned[pl.ds(pl.multiple_of(base + row, 8), 16), :], RECORD_TOP)

    wide_lane = lax.broadcasted_iota(jnp.int32, (16, 128), 1)

    @pl.loop(0, 9)
    def _(k):
        low = turned[pl.ds(pl.multiple_of(their_base + 16 * k, 8), 16), :]
        high = turned[pl.ds(pl.multiple_of(their_base + 136 + 16 * k, 8), 16), :]
        rec_z[k] = root_code(jnp.where(wide_lane < 64, low, pltpu.roll(high, 64, 1)), RECORD_TOP)

    rec_z_copy.start()
    for side in range(2):
        rec_near_copy(side).start()

    for load in loads[:4]:
        load.wait()

    @pl.loop(1, CHUNKS)
    def _(j):
        encode(j)

        @pl.when(j < AHEAD)
        def _():
            z_copy(j).start()

    for load in loads[4:]:
        load.wait()

    @pl.loop(0, CHUNKS)
    def _(j):
        for i in range(CHUNK):
            row = pl.multiple_of(8 * (CHUNK * j + i), 8)
            for f in range(4):
                block = state[f, 7:15, pl.ds(row + 8, 8), :].reshape(64, 128)
                near[j, CHUNK * f + i] = root_code(block, FIELD_TOP)
            near[j, CHUNK * 4 + i] = line_code(slope[7:15, pl.ds(row, 8), :].reshape(64, 128), SHAPE_TOP)
            near[j, CHUNK * 5 + i] = line_code(speed[7:15, pl.ds(row, 8), :].reshape(64, 128), SPEED_TOP)
        for side in range(2):
            near_copy(j, side).start()

    lane = lax.broadcasted_iota(jnp.int32, (8, 128), 1)
    sub = lax.broadcasted_iota(jnp.int32, (8, 128), 0)
    has = (jnp.where(q > 0, 1.0, 0.0), jnp.where(q < 15, 1.0, 0.0))

    def fill_source(shot):
        tag = jnp.zeros((8, 128), jnp.float32)
        for t in range(STEPS):
            tag = jnp.where((lane & 7) == t, wavelet[t, shot], tag)
        at_x = shot_x[shot] - 8 * q + 7
        at_y = shot_y[shot] - base

        @pl.loop(0, BLOCKS)
        def _(k):
            row = pl.multiple_of(8 * k, 8)
            for g in range(2):
                hit = ((sub + row) == at_y) & (((lane >> 3) + 16 * g) == at_x)
                inject[0, g, pl.ds(row, 8), :] = jnp.where(hit, tag, 0.0)

    def place_records(row, parts):
        low = pltpu.roll(parts[0], 120, 1) * has[0]
        mid = pltpu.roll(parts[1], 56, 1)
        high = pltpu.roll(parts[2], 120, 1) * has[1]
        inject[1, 0, pl.ds(row, 16), :] = jnp.where(wide_lane < 56, low, jnp.where(wide_lane < 120, mid, high))
        inject[1, 1, pl.ds(row, 16), :] = high

    def fill_near_records():
        @pl.loop(0, 17)
        def _(k):
            codes = (rec_near_in[0, k], rec_near[k], rec_near_in[1, k])
            place_records(pl.multiple_of(16 * k, 8), [root_value(c, RECORD_TOP) for c in codes])

    def fill_far_records():
        @pl.loop(0, 9)
        def _(k):
            parts = [root_value(c, RECORD_TOP) for c in (rec_far_in[0, k], rec_z_in[k], rec_far_in[1, k])]
            place_records(pl.multiple_of(16 * k, 8), parts)

        @pl.loop(0, 9)
        def _(k):
            parts = [root_value(c, RECORD_TOP) for c in (rec_far_in[0, k], rec_z_in[k], rec_far_in[1, k])]
            place_records(pl.multiple_of(136 + 16 * k, 8), [pltpu.roll(p, 64, 1) for p in parts])

    for f in range(4):
        state[f, :, 0:8, :] = jnp.zeros((WIDE, 8, 128), jnp.float32)
        state[f, :, ROWS + 8 : ROWS + 16, :] = jnp.zeros((WIDE, 8, 128), jnp.float32)

    def imaged(shot):
        inside = jnp.float32(0.0)
        for i in range(8):
            inside = inside + jnp.where(aperture[i, shot] == q, 1.0, 0.0)
        scale = []
        for t in range(1, 9):
            hit = jnp.float32(0.0)
            for i in range(4):
                hit = hit + jnp.where(snap_steps[i] == t, 1.0, 0.0)
            scale.append(hit * inside)
        return scale

    own_scale, other_scale = imaged(s), imaged(across)

    def rounded(x):
        return x.astype(jnp.bfloat16).astype(jnp.float32)

    def layers(n, size):
        found = []
        for low, high in ((n, 7), (7, 15), (15, WIDE - n)):
            found += [(x, min(x + size, high)) for x in range(low, high, size)]
        return found

    def one_step(phase, n, k, blocks, size):
        tall = 8 * blocks
        row = pl.multiple_of(8 * k, 8)
        here, flat_here = pl.ds(pl.multiple_of(row + 8, 8), tall), pl.ds(row, tall)
        for x0, x1 in layers(n, size):
            count = x1 - x0
            at = lax.broadcasted_iota(jnp.int32, (count, tall, 128), 2)
            for w in range(2):
                old, now = 2 * w + (n - 1) % 2, 2 * w + n % 2
                entry = n - 1 if w == 0 else STEPS - n
                big = state[now, x0 - 1 : x1 + 1, here, :]
                mid = big[1:-1]
                lateral = big[:-2] + big[2:]
                beside = state[now, x0:x1, pl.ds(row + 7, tall), :] + state[now, x0:x1, pl.ds(row + 9, tall), :]
                lateral = lateral + beside - 4.0 * mid
                added = jnp.stack([
                    pltpu.roll(inject[w, x // 16, flat_here, :], (128 - 8 * (x % 16) - entry) % 128, 1)
                    for x in range(x0, x1)
                ])
                up = jnp.where(at == 0, added, pltpu.roll(mid, 1, 2))
                down = jnp.where(at == 127, 0.0, pltpu.roll(mid, 127, 2))
                twice = 2.0 * mid
                new = twice - state[old, x0:x1, here, :]
                new = new + slope[x0:x1, flat_here, :] * lateral + speed[x0:x1, flat_here, :] * (up + down - twice)
                state[old, x0:x1, here, :] = new
                if not 7 <= x0 < 15:
                    continue
                for i in range(blocks):
                    flat = new[:, 8 * i : 8 * i + 8, :].reshape(8 * count, 128)
                    part = pl.ds(8 * (x0 - 7), 8 * count)
                    if phase == 0 and w == 0:
                        snap_u[n, k + i, part] = flat.astype(jnp.bfloat16)
                    elif phase == 0:
                        snap_w[STEPS - n, k + i, part] = flat
                    elif w == 0:
                        total[k + i, part] += other_scale[n] * rounded(flat) * snap_w[n, k + i, part]
                    else:
                        level = STEPS - n
                        total[k + i, part] += own_scale[level] * flat * snap_u[level, k + i, part].astype(jnp.float32)

    def spread(f, rows, low, high, mid=None):
        state[f, 0:7, rows, :] = (root_value(low, FIELD_TOP) * has[0]).reshape(8, 8, 128)[1:8]
        state[f, 15:22, rows, :] = (root_value(high, FIELD_TOP) * has[1]).reshape(8, 8, 128)[0:7]
        if mid is not None:
            mid = root_value(mid, FIELD_TOP)
            state[f, 7:15, rows, :] = mid.reshape(8, 8, 128)
        return mid

    def open_near(j):
        @pl.loop(0, CHUNK)
        def _(i):
            k = CHUNK * j + i
            row = pl.multiple_of(8 * k, 8)
            rows = pl.ds(pl.multiple_of(row + 8, 8), 8)
            for f in range(4):
                spread(f, rows, near_in[0, j, CHUNK * f + i], near_in[1, j, CHUNK * f + i])
            snap_u[0, k] = state[1, 7:15, rows, :].reshape(64, 128).astype(jnp.bfloat16)
            snap_w[STEPS, k] = state[3, 7:15, rows, :].reshape(64, 128)
            for side, cut, into in ((0, slice(1, 8), slice(0, 7)), (1, slice(0, 7), slice(15, 22))):
                tilt = line_value(near_in[side, j, CHUNK * 4 + i], SHAPE_TOP)
                fast = line_value(near_in[side, j, CHUNK * 5 + i], SPEED_TOP) * has[side]
                speed[into, pl.ds(row, 8), :] = fast.reshape(8, 8, 128)[cut]
                slope[into, pl.ds(row, 8), :] = (fast * (1.0 + 2.0 * tilt)).reshape(8, 8, 128)[cut]
            fast = speed[7:15, pl.ds(row, 8), :]
            slope[7:15, pl.ds(row, 8), :] = fast * (1.0 + 2.0 * slope[7:15, pl.ds(row, 8), :])

    def open_far(j):
        @pl.loop(0, CHUNK)
        def _(i):
            k = CHUNK * j + i
            rows = pl.ds(pl.multiple_of(8 * k + 8, 8), 8)
            mids = []
            for f in range(4):
                at = CHUNK * f + i
                mids.append(spread(f, rows, far_in[0, j, at], far_in[1, j, at], z_in[j, at]))
            total[k] = (
                other_scale[0] * rounded(mids[1]) * snap_w[0, k]
                + own_scale[STEPS] * mids[3] * snap_u[STEPS, k].astype(jnp.float32)
            )

    def advance(phase, j):
        for n in range(1, STEPS + 1):
            first = jnp.maximum(CHUNK * j - n, 0)
            last = jnp.where(j == CHUNKS - 1, BLOCKS, jnp.maximum(CHUNK * j + CHUNK - n, 0))
            threes = (last - first) // CHUNK

            @pl.loop(0, threes)
            def _(i):
                one_step(phase, n, first + CHUNK * i, CHUNK, 4)

            @pl.loop(first + CHUNK * threes, last)
            def _(k):
                one_step(phase, n, k, 1, 8)

    mine = lax.rem(s, 8)

    def sum_copy(k):
        part = lax.rem(s + k, 8)
        return remote(sum_out.at[part], sums.at[k - 1], sum_send.at[k - 1], sum_recv.at[k - 1], (8 * half + part, q))

    def send_sums(k):
        part = lax.rem(s + k, 8)
        for i in range(4):
            sum_out[part, i] = long_code(total[half + 4 * part + i])
        sum_copy(k).start()

    fill_source(s)
    for side in range(2):
        rec_near_copy(1 - side).wait_recv()
    fill_near_records()

    @pl.loop(0, CHUNKS)
    def _(j):
        for side in range(2):
            near_copy(j, 1 - side).wait_recv()
        open_near(j)
        advance(0, j)

        @pl.when((lax.rem(j, 3) == 2) & (j // 3 + AHEAD < SENT_EARLY))
        def _():
            z_copy(j // 3).wait_send()
            z_copy(j // 3 + AHEAD).start()

    rec_z_copy.wait_recv()
    for side in range(2):
        rec_far_copy(side).start()

    def pass_on(j):
        z_copy(j).wait_recv()
        for side in range(2):
            far_copy(j, side).start()

    @pl.loop(0, BESIDE)
    def _(j):
        pass_on(j)

    fill_source(across)
    for side in range(2):
        rec_far_copy(1 - side).wait_recv()
    fill_far_records()

    @pl.loop(0, CHUNKS + 1)
    def _(j):
        @pl.when((j >= BESIDE) & (j < CHUNKS))
        def _():
            pass_on(j)

        @pl.when((j >= SENT_EARLY - 2) & (j < CHUNKS - 2))
        def _():
            z_copy(j).wait_send()
            z_copy(j + 2).start()

        @pl.when(j > 0)
        def _():
            for side in range(2):
                far_copy(j - 1, 1 - side).wait_recv()
            open_far(j - 1)
            advance(1, j - 1)

    for k in (4, 3, 5, 2, 6, 1, 7):
        send_sums(k)
    for k in (1, 7, 2, 6, 3, 5, 4):
        sum_copy(k).wait_recv()
        for i in range(4):
            total[half + 4 * mine + i] += long_value(sums[k - 1, i])
    for i in range(4):
        out[:, 8 * i : 8 * i + 8, :] = total[half + 4 * mine + i].reshape(8, 8, 128)

    @pl.loop(0, CHUNKS)
    def _(j):
        @pl.when(((j >= SENT_EARLY - AHEAD) & (j < SENT_EARLY - 2)) | (j >= CHUNKS - 2))
        def _():
            z_copy(j).wait_send()
        for side in range(2):
            near_copy(j, side).wait_send()
            far_copy(j, side).wait_send()

    rec_z_copy.wait_send()
    for side in range(2):
        rec_near_copy(side).wait_send()
        rec_far_copy(side).wait_send()
    for k in range(1, 8):
        sum_copy(k).wait_send()


def on_device(*args):
    f32, i16 = jnp.float32, jnp.int16
    dma = pltpu.SemaphoreType.DMA
    fields = (args[0], args[1], args[2], args[3])
    records, speed, shape = args[4], args[5], args[6]
    anywhere, smem = pl.BlockSpec(memory_space=pl.ANY), pl.BlockSpec(memory_space=pltpu.SMEM)
    vmem = pl.BlockSpec(memory_space=pltpu.VMEM)
    return pl.pallas_call(
        kernel,
        out_shape=jax.ShapeDtypeStruct((8, 32, 128), f32),
        in_specs=[anywhere] * 6 + [vmem] + [smem] * 5,
        out_specs=vmem,
        scratch_shapes=[
            pltpu.VMEM((4, WIDE, ROWS + 16, 128), f32),
            pltpu.VMEM((WIDE, ROWS, 128), f32),
            pltpu.VMEM((WIDE, ROWS, 128), f32),
            pltpu.VMEM((8, BLOCKS, 64, 128), jnp.bfloat16),
            pltpu.VMEM((8, BLOCKS, 64, 128), f32),
            pltpu.VMEM((BLOCKS, 64, 128), f32),
            pltpu.VMEM((4, 8, ROWS, 128), f32),
            pltpu.VMEM((CHUNKS, 4 * CHUNK, 64, 128), i16),
            pltpu.VMEM((CHUNKS, 4 * CHUNK, 64, 128), i16),
            pltpu.VMEM((CHUNKS, 6 * CHUNK, 64, 128), i16),
            pltpu.VMEM((2, CHUNKS, 6 * CHUNK, 64, 128), i16),
            pltpu.VMEM((2, CHUNKS, 4 * CHUNK, 64, 128), i16),
            pltpu.VMEM((2, 2, 280, 128), f32),
            pltpu.VMEM((16, 8, 512), f32),
            pltpu.VMEM((528, 128), f32),
            pltpu.VMEM((9, 16, 128), i16),
            pltpu.VMEM((17, 16, 128), i16),
            pltpu.VMEM((9, 16, 128), i16),
            pltpu.VMEM((2, 17, 16, 128), i16),
            pltpu.VMEM((2, 9, 16, 128), i16),
            pltpu.VMEM((8, 4, 64, 128), i16),
            pltpu.VMEM((7, 4, 64, 128), i16),
            dma((14,)),
            dma((CHUNKS,)),
            dma((CHUNKS,)),
            dma((2, CHUNKS)),
            dma((2, CHUNKS)),
            dma((2, CHUNKS)),
            dma((2, CHUNKS)),
            dma,
            dma,
            dma((2,)),
            dma((2,)),
            dma((2,)),
            dma((2,)),
            dma((7,)),
            dma((7,)),
        ],
        compiler_params=pltpu.CompilerParams(
            collective_id=0, has_side_effects=True, vmem_limit_bytes=62 * 1024 * 1024
        ),
    )(*fields, speed, shape, records, args[7].T, args[8], args[9], args[10].T, args[11])


def solution(mesh):
    in_specs = (
        P("shot", "xy", None, None),
        P("shot", "xy", None, None),
        P("shot", "xy", None, None),
        P("shot", "xy", None, None),
        P("shot", None, "xy", None),
        P("xy", None, None),
        P("xy", None, None),
        P(),
        P(),
        P(),
        P(),
        P(),
    )
    return jax.shard_map(
        on_device, mesh=mesh, in_specs=in_specs, out_specs=P("xy", "shot", None), check_vma=False
    )
```

```python
import functools

import jax
import jax.numpy as jnp
from jax import lax
from jax.experimental import pallas as pl
from jax.experimental.pallas import tpu as pltpu
from jax.sharding import PartitionSpec as P

MESH = pl.DeviceIdType.MESH
TOP = 32767.0
BLOCKS = 33
CHUNK = 3
CHUNKS = BLOCKS // CHUNK
ROWS = 8 * BLOCKS
STEPS = 7
BESIDE = 5
SENT_EARLY = 9
AHEAD = 6
WIDE = 22
FIELD_TOP = 6.0
RECORD_TOP = 12.0
SPEED_TOP = 0.25
SHAPE_TOP = 0.3
SUM_TOP = 2.0**30


def root_code(x, top):
    size = jnp.sqrt(jnp.sqrt(jnp.abs(x) * (1.0 / top))) * TOP
    size = jnp.minimum(jnp.round(size), TOP)
    return jnp.where(x < 0.0, -size, size).astype(jnp.int32).astype(jnp.int16)


def root_value(code, top):
    part = code.astype(jnp.int32).astype(jnp.float32) * (1.0 / TOP)
    return (part * part) * (part * jnp.abs(part)) * top


def long_code(x):
    size = jnp.abs(x) * (1.0 / SUM_TOP)
    for _ in range(4):
        size = jnp.sqrt(size)
    size = jnp.minimum(jnp.round(size * TOP), TOP)
    return jnp.where(x < 0.0, -size, size).astype(jnp.int32).astype(jnp.int16)


def long_value(code):
    part = code.astype(jnp.int32).astype(jnp.float32) * (1.0 / TOP)
    power = jnp.abs(part)
    for _ in range(4):
        power = power * power
    return jnp.where(part < 0.0, -power, power) * SUM_TOP


def line_code(x, top):
    return jnp.round(x * (TOP / top)).astype(jnp.int32).astype(jnp.int16)


def line_value(code, top):
    return code.astype(jnp.int32).astype(jnp.float32) * (top / TOP)


def kernel(
    fields0, fields1, fields2, fields3, speed_hbm, shape_hbm, records, wavelet, shot_x, shot_y, aperture, snap_steps,
    out,
    state, slope, speed, snap_u, snap_w, total, stage, z_out, z_in, near, near_in, far_in,
    inject, marks, turned, rec_z, rec_near, rec_z_in, rec_near_in, rec_far_in, sum_out, sums,
    in_sem, z_send, z_recv, near_send, near_recv, far_send, far_recv,
    rz_send, rz_recv, rn_send, rn_recv, rf_send, rf_recv, sum_send, sum_recv,
):
    fields = (fields0, fields1, fields2, fields3)
    s, q = lax.axis_index("shot"), lax.axis_index("xy")
    half = s // 8
    across = lax.rem(s + 8, 16)
    left, right = lax.rem(q + 15, 16), lax.rem(q + 1, 16)
    sides = ((s, left), (s, right))
    base = pl.multiple_of(248 * half, 8)
    their_base = pl.multiple_of(248 * (1 - half), 8)

    firsts, loads = [], []
    tall = 8 * CHUNK
    for f in range(4):
        theirs = fields[f].at[0]
        rest = pl.ds(pl.multiple_of(their_base + tall, 8), ROWS - tall)
        firsts.append(pltpu.make_async_copy(theirs.at[:, pl.ds(their_base, tall), :], stage.at[f, :, pl.ds(0, tall), :], in_sem.at[10 + f]))
        loads.append(pltpu.make_async_copy(theirs.at[:, rest, :], stage.at[f, :, pl.ds(tall, ROWS - tall), :], in_sem.at[f]))
    for f in range(4):
        loads.append(pltpu.make_async_copy(fields[f].at[0, :, pl.ds(base, ROWS), :], state.at[f, pl.ds(7, 8), pl.ds(8, ROWS), :], in_sem.at[4 + f]))
    loads.append(pltpu.make_async_copy(shape_hbm.at[:, pl.ds(base, ROWS), :], slope.at[pl.ds(7, 8)], in_sem.at[8]))
    loads.append(pltpu.make_async_copy(speed_hbm.at[:, pl.ds(base, ROWS), :], speed.at[pl.ds(7, 8)], in_sem.at[9]))
    for load in firsts + loads[:4]:
        load.start()

    barrier = pltpu.get_barrier_semaphore()
    peers = [(across, q), *sides]
    for k in range(1, 8):
        peers.append((8 * half + lax.rem(s + k, 8), q))
    for peer in peers:
        pl.semaphore_signal(barrier, inc=1, device_id=peer, device_id_type=MESH)

    def remote(src, dst, send, recv, target):
        return pltpu.make_async_remote_copy(
            src_ref=src, dst_ref=dst, send_sem=send, recv_sem=recv, device_id=target, device_id_type=MESH
        )

    def z_copy(j):
        return remote(z_out.at[j], z_in.at[j], z_send.at[j], z_recv.at[j], (across, q))

    def near_copy(j, side):
        return remote(near.at[j], near_in.at[1 - side, j], near_send.at[side, j], near_recv.at[1 - side, j], sides[side])

    def far_copy(j, side):
        return remote(z_in.at[j], far_in.at[1 - side, j], far_send.at[side, j], far_recv.at[1 - side, j], sides[side])

    def arrived(copy_of, j, side):
        return copy_of(j, 1 - side)

    def rec_near_copy(side):
        return remote(rec_near, rec_near_in.at[1 - side], rn_send.at[side], rn_recv.at[1 - side], sides[side])

    def rec_far_copy(side):
        return remote(rec_z_in, rec_far_in.at[1 - side], rf_send.at[side], rf_recv.at[1 - side], sides[side])

    rec_z_copy = remote(rec_z, rec_z_in, rz_send, rz_recv, (across, q))

    def encode(j):
        for f in range(4):
            for i in range(CHUNK):
                row = pl.multiple_of(8 * (CHUNK * j + i), 8)
                block = stage[f, :, pl.ds(row, 8), :].reshape(64, 128)
                z_out[j, CHUNK * f + i] = root_code(block, FIELD_TOP)

    for load in firsts:
        load.wait()
    for load in loads[4:]:
        load.start()
    encode(0)
    pl.semaphore_wait(barrier, len(peers))
    z_copy(0).start()

    marks[...] = jnp.zeros_like(marks)
    for t in range(STEPS):
        for x in range(8):
            marks[x, t : t + 1, :] = records[0, t, x : x + 1, :]
    turned[pl.ds(512, 16)] = jnp.zeros((16, 128), jnp.float32)
    turned[pl.ds(0, 512)] = jnp.transpose(marks[...].reshape(128, 512), (1, 0))

    @pl.loop(0, 17)
    def _(k):
        row = 16 * k
        rec_near[k] = root_code(turned[pl.ds(pl.multiple_of(base + row, 8), 16), :], RECORD_TOP)

    wide_lane = lax.broadcasted_iota(jnp.int32, (16, 128), 1)

    @pl.loop(0, 9)
    def _(k):
        low = turned[pl.ds(pl.multiple_of(their_base + 16 * k, 8), 16), :]
        high = turned[pl.ds(pl.multiple_of(their_base + 136 + 16 * k, 8), 16), :]
        rec_z[k] = root_code(jnp.where(wide_lane < 64, low, pltpu.roll(high, 64, 1)), RECORD_TOP)

    rec_z_copy.start()
    for side in range(2):
        rec_near_copy(side).start()

    for load in loads[:4]:
        load.wait()

    @pl.loop(1, CHUNKS)
    def _(j):
        encode(j)

        @pl.when(j < AHEAD)
        def _():
            z_copy(j).start()

    for load in loads[4:]:
        load.wait()

    @pl.loop(0, CHUNKS)
    def _(j):
        for i in range(CHUNK):
            row = pl.multiple_of(8 * (CHUNK * j + i), 8)
            for f in range(4):
                block = state[f, 7:15, pl.ds(row + 8, 8), :].reshape(64, 128)
                near[j, CHUNK * f + i] = root_code(block, FIELD_TOP)
            near[j, CHUNK * 4 + i] = line_code(slope[7:15, pl.ds(row, 8), :].reshape(64, 128), SHAPE_TOP)
            near[j, CHUNK * 5 + i] = line_code(speed[7:15, pl.ds(row, 8), :].reshape(64, 128), SPEED_TOP)
        for side in range(2):
            near_copy(j, side).start()

    lane = lax.broadcasted_iota(jnp.int32, (8, 128), 1)
    sub = lax.broadcasted_iota(jnp.int32, (8, 128), 0)
    has = (jnp.where(q > 0, 1.0, 0.0), jnp.where(q < 15, 1.0, 0.0))

    def fill_source(shot):
        tag = jnp.zeros((8, 128), jnp.float32)
        for t in range(STEPS):
            tag = jnp.where((lane & 7) == t, wavelet[t, shot], tag)
        at_x = shot_x[shot] - 8 * q + 7
        at_y = shot_y[shot] - base

        @pl.loop(0, BLOCKS)
        def _(k):
            row = pl.multiple_of(8 * k, 8)
            for g in range(2):
                hit = ((sub + row) == at_y) & (((lane >> 3) + 16 * g) == at_x)
                inject[0, g, pl.ds(row, 8), :] = jnp.where(hit, tag, 0.0)

    def place_records(row, parts):
        low = pltpu.roll(parts[0], 120, 1) * has[0]
        mid = pltpu.roll(parts[1], 56, 1)
        high = pltpu.roll(parts[2], 120, 1) * has[1]
        inject[1, 0, pl.ds(row, 16), :] = jnp.where(wide_lane < 56, low, jnp.where(wide_lane < 120, mid, high))
        inject[1, 1, pl.ds(row, 16), :] = high

    def fill_near_records():
        @pl.loop(0, 17)
        def _(k):
            codes = (rec_near_in[0, k], rec_near[k], rec_near_in[1, k])
            place_records(pl.multiple_of(16 * k, 8), [root_value(c, RECORD_TOP) for c in codes])

    def fill_far_records():
        @pl.loop(0, 9)
        def _(k):
            parts = [root_value(c, RECORD_TOP) for c in (rec_far_in[0, k], rec_z_in[k], rec_far_in[1, k])]
            place_records(pl.multiple_of(16 * k, 8), parts)

        @pl.loop(0, 9)
        def _(k):
            parts = [root_value(c, RECORD_TOP) for c in (rec_far_in[0, k], rec_z_in[k], rec_far_in[1, k])]
            place_records(pl.multiple_of(136 + 16 * k, 8), [pltpu.roll(p, 64, 1) for p in parts])

    for f in range(4):
        state[f, :, 0:8, :] = jnp.zeros((WIDE, 8, 128), jnp.float32)
        state[f, :, ROWS + 8 : ROWS + 16, :] = jnp.zeros((WIDE, 8, 128), jnp.float32)

    def imaged(shot):
        inside = jnp.float32(0.0)
        for i in range(8):
            inside = inside + jnp.where(aperture[i, shot] == q, 1.0, 0.0)
        scale = []
        for t in range(1, 9):
            hit = jnp.float32(0.0)
            for i in range(4):
                hit = hit + jnp.where(snap_steps[i] == t, 1.0, 0.0)
            scale.append(hit * inside)
        return scale

    own_scale, other_scale = imaged(s), imaged(across)

    def rounded(x):
        return x.astype(jnp.bfloat16).astype(jnp.float32)

    def layers(n, size):
        found = []
        for low, high in ((n, 7), (7, 15), (15, WIDE - n)):
            found += [(x, min(x + size, high)) for x in range(low, high, size)]
        return found

    def one_step(phase, n, k, blocks, size):
        tall = 8 * blocks
        row = pl.multiple_of(8 * k, 8)
        here, flat_here = pl.ds(pl.multiple_of(row + 8, 8), tall), pl.ds(row, tall)
        for x0, x1 in layers(n, size):
            count = x1 - x0
            at = lax.broadcasted_iota(jnp.int32, (count, tall, 128), 2)
            for w in range(2):
                old, now = 2 * w + (n - 1) % 2, 2 * w + n % 2
                entry = n - 1 if w == 0 else STEPS - n
                big = state[now, x0 - 1 : x1 + 1, here, :]
                mid = big[1:-1]
                lateral = big[:-2] + big[2:]
                beside = state[now, x0:x1, pl.ds(row + 7, tall), :] + state[now, x0:x1, pl.ds(row + 9, tall), :]
                lateral = lateral + beside - 4.0 * mid
                added = jnp.stack([
                    pltpu.roll(inject[w, x // 16, flat_here, :], (128 - 8 * (x % 16) - entry) % 128, 1)
                    for x in range(x0, x1)
                ])
                up = jnp.where(at == 0, added, pltpu.roll(mid, 1, 2))
                down = jnp.where(at == 127, 0.0, pltpu.roll(mid, 127, 2))
                twice = 2.0 * mid
                new = twice - state[old, x0:x1, here, :]
                new = new + slope[x0:x1, flat_here, :] * lateral + speed[x0:x1, flat_here, :] * (up + down - twice)
                state[old, x0:x1, here, :] = new
                if not 7 <= x0 < 15:
                    continue
                for i in range(blocks):
                    flat = new[:, 8 * i : 8 * i + 8, :].reshape(8 * count, 128)
                    part = pl.ds(8 * (x0 - 7), 8 * count)
                    if phase == 0 and w == 0:
                        snap_u[n, k + i, part] = flat.astype(jnp.bfloat16)
                    elif phase == 0:
                        snap_w[STEPS - n, k + i, part] = flat
                    elif w == 0:
                        total[k + i, part] += other_scale[n] * rounded(flat) * snap_w[n, k + i, part]
                    else:
                        level = STEPS - n
                        total[k + i, part] += own_scale[level] * flat * snap_u[level, k + i, part].astype(jnp.float32)

    def spread(f, rows, low, high, mid=None):
        state[f, 0:7, rows, :] = (root_value(low, FIELD_TOP) * has[0]).reshape(8, 8, 128)[1:8]
        state[f, 15:22, rows, :] = (root_value(high, FIELD_TOP) * has[1]).reshape(8, 8, 128)[0:7]
        if mid is not None:
            mid = root_value(mid, FIELD_TOP)
            state[f, 7:15, rows, :] = mid.reshape(8, 8, 128)
        return mid

    def open_near(j):
        @pl.loop(0, CHUNK)
        def _(i):
            k = CHUNK * j + i
            row = pl.multiple_of(8 * k, 8)
            rows = pl.ds(pl.multiple_of(row + 8, 8), 8)
            for f in range(4):
                spread(f, rows, near_in[0, j, CHUNK * f + i], near_in[1, j, CHUNK * f + i])
            snap_u[0, k] = state[1, 7:15, rows, :].reshape(64, 128).astype(jnp.bfloat16)
            snap_w[STEPS, k] = state[3, 7:15, rows, :].reshape(64, 128)
            for side, cut, into in ((0, slice(1, 8), slice(0, 7)), (1, slice(0, 7), slice(15, 22))):
                tilt = line_value(near_in[side, j, CHUNK * 4 + i], SHAPE_TOP)
                fast = line_value(near_in[side, j, CHUNK * 5 + i], SPEED_TOP) * has[side]
                speed[into, pl.ds(row, 8), :] = fast.reshape(8, 8, 128)[cut]
                slope[into, pl.ds(row, 8), :] = (fast * (1.0 + 2.0 * tilt)).reshape(8, 8, 128)[cut]
            fast = speed[7:15, pl.ds(row, 8), :]
            slope[7:15, pl.ds(row, 8), :] = fast * (1.0 + 2.0 * slope[7:15, pl.ds(row, 8), :])

    def open_far(j):
        @pl.loop(0, CHUNK)
        def _(i):
            k = CHUNK * j + i
            rows = pl.ds(pl.multiple_of(8 * k + 8, 8), 8)
            mids = []
            for f in range(4):
                at = CHUNK * f + i
                mids.append(spread(f, rows, far_in[0, j, at], far_in[1, j, at], z_in[j, at]))
            total[k] = (
                other_scale[0] * rounded(mids[1]) * snap_w[0, k]
                + own_scale[STEPS] * mids[3] * snap_u[STEPS, k].astype(jnp.float32)
            )

    def advance(phase, j):
        for n in range(1, STEPS + 1):
            first = jnp.maximum(CHUNK * j - n, 0)
            last = jnp.where(j == CHUNKS - 1, BLOCKS, jnp.maximum(CHUNK * j + CHUNK - n, 0))
            threes = (last - first) // CHUNK

            @pl.loop(0, threes)
            def _(i):
                one_step(phase, n, first + CHUNK * i, CHUNK, 4)

            @pl.loop(first + CHUNK * threes, last)
            def _(k):
                one_step(phase, n, k, 1, 8)

    mine = lax.rem(s, 8)

    def sum_copy(k):
        part = lax.rem(s + k, 8)
        return remote(sum_out.at[part], sums.at[k - 1], sum_send.at[k - 1], sum_recv.at[k - 1], (8 * half + part, q))

    def send_sums(k):
        part = lax.rem(s + k, 8)
        for i in range(4):
            sum_out[part, i] = long_code(total[half + 4 * part + i])
        sum_copy(k).start()

    fill_source(s)
    for side in range(2):
        rec_near_copy(1 - side).wait_recv()
    fill_near_records()

    @pl.loop(0, CHUNKS)
    def _(j):
        for side in range(2):
            near_copy(j, 1 - side).wait_recv()
        open_near(j)
        advance(0, j)

        @pl.when((lax.rem(j, 3) == 2) & (j // 3 + AHEAD < SENT_EARLY))
        def _():
            z_copy(j // 3).wait_send()
            z_copy(j // 3 + AHEAD).start()

    rec_z_copy.wait_recv()
    for side in range(2):
        rec_far_copy(side).start()

    def pass_on(j):
        z_copy(j).wait_recv()
        for side in range(2):
            far_copy(j, side).start()

    @pl.loop(0, BESIDE)
    def _(j):
        pass_on(j)

    fill_source(across)
    for side in range(2):
        rec_far_copy(1 - side).wait_recv()
    fill_far_records()

    @pl.loop(0, CHUNKS + 1)
    def _(j):
        @pl.when((j >= BESIDE) & (j < CHUNKS))
        def _():
            pass_on(j)

        @pl.when((j >= SENT_EARLY - 2) & (j < CHUNKS - 2))
        def _():
            z_copy(j).wait_send()
            z_copy(j + 2).start()

        @pl.when(j > 0)
        def _():
            for side in range(2):
                far_copy(j - 1, 1 - side).wait_recv()
            open_far(j - 1)
            advance(1, j - 1)

    for k in (4, 3, 5, 2, 6, 1, 7):
        send_sums(k)
    for k in (1, 7, 2, 6, 3, 5, 4):
        sum_copy(k).wait_recv()
        for i in range(4):
            total[half + 4 * mine + i] += long_value(sums[k - 1, i])
    for i in range(4):
        out[:, 8 * i : 8 * i + 8, :] = total[half + 4 * mine + i].reshape(8, 8, 128)

    @pl.loop(0, CHUNKS)
    def _(j):
        @pl.when(((j >= SENT_EARLY - AHEAD) & (j < SENT_EARLY - 2)) | (j >= CHUNKS - 2))
        def _():
            z_copy(j).wait_send()
        for side in range(2):
            near_copy(j, side).wait_send()
            far_copy(j, side).wait_send()

    rec_z_copy.wait_send()
    for side in range(2):
        rec_near_copy(side).wait_send()
        rec_far_copy(side).wait_send()
    for k in range(1, 8):
        sum_copy(k).wait_send()


def on_device(*args):
    f32, i16 = jnp.float32, jnp.int16
    dma = pltpu.SemaphoreType.DMA
    fields = (args[0], args[1], args[2], args[3])
    records, speed, shape = args[4], args[5], args[6]
    anywhere, smem = pl.BlockSpec(memory_space=pl.ANY), pl.BlockSpec(memory_space=pltpu.SMEM)
    vmem = pl.BlockSpec(memory_space=pltpu.VMEM)
    return pl.pallas_call(
        kernel,
        out_shape=jax.ShapeDtypeStruct((8, 32, 128), f32),
        in_specs=[anywhere] * 6 + [vmem] + [smem] * 5,
        out_specs=vmem,
        scratch_shapes=[
            pltpu.VMEM((4, WIDE, ROWS + 16, 128), f32),
            pltpu.VMEM((WIDE, ROWS, 128), f32),
            pltpu.VMEM((WIDE, ROWS, 128), f32),
            pltpu.VMEM((8, BLOCKS, 64, 128), jnp.bfloat16),
            pltpu.VMEM((8, BLOCKS, 64, 128), f32),
            pltpu.VMEM((BLOCKS, 64, 128), f32),
            pltpu.VMEM((4, 8, ROWS, 128), f32),
            pltpu.VMEM((CHUNKS, 4 * CHUNK, 64, 128), i16),
            pltpu.VMEM((CHUNKS, 4 * CHUNK, 64, 128), i16),
            pltpu.VMEM((CHUNKS, 6 * CHUNK, 64, 128), i16),
            pltpu.VMEM((2, CHUNKS, 6 * CHUNK, 64, 128), i16),
            pltpu.VMEM((2, CHUNKS, 4 * CHUNK, 64, 128), i16),
            pltpu.VMEM((2, 2, 280, 128), f32),
            pltpu.VMEM((16, 8, 512), f32),
            pltpu.VMEM((528, 128), f32),
            pltpu.VMEM((9, 16, 128), i16),
            pltpu.VMEM((17, 16, 128), i16),
            pltpu.VMEM((9, 16, 128), i16),
            pltpu.VMEM((2, 17, 16, 128), i16),
            pltpu.VMEM((2, 9, 16, 128), i16),
            pltpu.VMEM((8, 4, 64, 128), i16),
            pltpu.VMEM((7, 4, 64, 128), i16),
            dma((14,)),
            dma((CHUNKS,)),
            dma((CHUNKS,)),
            dma((2, CHUNKS)),
            dma((2, CHUNKS)),
            dma((2, CHUNKS)),
            dma((2, CHUNKS)),
            dma,
            dma,
            dma((2,)),
            dma((2,)),
            dma((2,)),
            dma((2,)),
            dma((7,)),
            dma((7,)),
        ],
        compiler_params=pltpu.CompilerParams(
            collective_id=0, has_side_effects=True, vmem_limit_bytes=62 * 1024 * 1024
        ),
    )(*fields, speed, shape, records, args[7].T, args[8], args[9], args[10].T, args[11])


def solution(mesh):
    in_specs = (
        P("shot", "xy", None, None),
        P("shot", "xy", None, None),
        P("shot", "xy", None, None),
        P("shot", "xy", None, None),
        P("shot", None, "xy", None),
        P("xy", None, None),
        P("xy", None, None),
        P(),
        P(),
        P(),
        P(),
        P(),
    )
    return jax.shard_map(
        on_device, mesh=mesh, in_specs=in_specs, out_specs=P("xy", "shot", None), check_vma=False
    )
```
